512 devices in a mesh: ch: 512 (over x, y, z, core).
Axes of the slice: x: 4, y: 4, z: 16, core: 2. Of those that a mesh axis runs over, the one named last changes fastest.
Arguments:
- strain: bfloat16 [8192, 6144], P('ch'), may hold values from -12 to 12
- band_start: int32 [1], replicated, may hold values from 0 to 255
- sketch_seed: int32 [1], replicated, may hold values from 0 to 999999
Outputs:
- modes: float32 [8192, 2, 16, 128], P('ch')
- factor: float32 [2, 16, 16, 128], replicated
The draws below stay inside these ranges and needn't reach their ends.
All inputs are finite; a program needn't handle non-finite values.
Results may differ from the reference program's by a relative error of at most 0.0003.
The reference program's roundings to bfloat16 on the way (of `table`) count: a program that leaves them out, or rounds other values in their place, can miss the bound.
Values sent between devices are 32-bit elements; how exact they have to be, the bound alone decides.
A program may use at most 64 MiB of HBM per device.

```python
import math
import jax
import jax.numpy as jnp
from jax import lax

SEGMENTS = 24
SEG_LEN = 256
LINES = 128
SKETCH = 16
CHANNELS = 8192
SAMPLES = 6144


def draw_strain(key, part):
    key = jax.random.fold_in(key, 11)
    noise_key, gain_key = jax.random.split(key)
    positions = jnp.arange(CHANNELS, dtype=jnp.float32) / CHANNELS
    trend_gain = jnp.power(3.0, positions)
    samples_noise = jax.random.normal(noise_key, (CHANNELS, SAMPLES), jnp.float32)
    log_spread = math.log(10.0)
    channel_gain = jnp.exp(jax.random.uniform(gain_key, (CHANNELS,), jnp.float32) * log_spread) * trend_gain * 0.4
    return jnp.clip(samples_noise * channel_gain[:, None], -12.0, 12.0).astype(jnp.bfloat16)


def setup_inputs(seed: int = 0) -> dict:
    splits = jax.random.split(jax.random.key(seed), 4)
    return {
        "strain": draw_strain(jax.random.fold_in(splits[3], 71), 0),
        "band_start": jax.random.randint(splits[1], (1,), 0, SEG_LEN).astype(jnp.int32),
        "sketch_seed": jax.random.randint(splits[2], (1,), 0, 1000000).astype(jnp.int32),
    }


def dft_table(band_start, segment_length, line_count):
    times_idx = jnp.arange(segment_length, dtype=jnp.int32)[:, None]
    line_ids = band_start[0] + jnp.arange(line_count, dtype=jnp.int32)[None, :]
    residues = times_idx * line_ids % segment_length
    phases = 2.0 * math.pi / segment_length * residues.astype(jnp.float32)
    window = 0.5 - 0.5 * jnp.cos(2.0 * math.pi / segment_length * times_idx.astype(jnp.float32))
    weighting = window / math.sqrt(3.0 * segment_length / 8.0)
    return jnp.concatenate([weighting * jnp.cos(phases), -weighting * jnp.sin(phases)], axis=1).astype(jnp.bfloat16)

def sketch_signs(first_channel, count, sketch_seed, sketch):
    channel_ids = first_channel + jnp.arange(count, dtype=jnp.int32)[:, None, None]
    column_ids = jnp.arange(sketch, dtype=jnp.int32)[None, :, None]
    halves = jnp.arange(2, dtype=jnp.int32)[None, None, :]
    hashed = (channel_ids * sketch + column_ids) * 2 + halves + sketch_seed[0] * 1000003
    hashed = hashed * -1640531535
    hashed = jnp.bitwise_xor(hashed, lax.shift_right_logical(hashed, jnp.full_like(hashed, 15)))
    hashed = hashed * 2146121005
    hashed = jnp.bitwise_xor(hashed, lax.shift_right_logical(hashed, jnp.full_like(hashed, 13)))
    sign_bits = jnp.bitwise_and(lax.shift_right_logical(hashed, jnp.full_like(hashed, 7)), 1)
    signs = (1 - 2 * sign_bits).astype(jnp.float32)
    return (signs[:, :, 0], signs[:, :, 1])

def contract(form, left_re, left_im, right_re, right_im, conjugate):

    def product(left, right):
        return jnp.einsum(form, left, right, precision=lax.Precision.HIGHEST)
    if conjugate:
        return (product(left_re, right_re) + product(left_im, right_im), product(left_re, right_im) - product(left_im, right_re))
    return (product(left_re, right_re) - product(left_im, right_im), product(left_re, right_im) + product(left_im, right_re))

def cholesky_upper(gram_re, gram_im):
    size = gram_re.shape[0]
    column_ids = jnp.arange(size, dtype=jnp.int32)[:, None]
    rows_re = []
    rows_im = []
    for column in range(size):
        accum_re = gram_re[column]
        accum_im = gram_im[column]
        if column > 0:
            prior_re = jnp.stack(rows_re)
            prior_im = jnp.stack(rows_im)
            top_re = prior_re[:, column, :][:, None, :]
            top_im = prior_im[:, column, :][:, None, :]
            accum_re = accum_re - lax.optimization_barrier(jnp.sum(top_re * prior_re + top_im * prior_im, axis=0))
            accum_im = accum_im - lax.optimization_barrier(jnp.sum(top_re * prior_im - top_im * prior_re, axis=0))
        diagonal = jnp.sqrt(accum_re[column])
        beyond = column_ids > column
        row_re = jnp.where(beyond, accum_re / diagonal[None, :], 0.0)
        row_re = jnp.where(column_ids == column, diagonal[None, :], row_re)
        row_im = jnp.where(beyond, accum_im / diagonal[None, :], 0.0)
        rows_re.append(row_re)
        rows_im.append(row_im)
    return (jnp.stack(rows_re), jnp.stack(rows_im))

def upper_inverse(upper_re, upper_im):
    size = upper_re.shape[0]
    column_ids = jnp.arange(size, dtype=jnp.int32)[:, None]
    lines = upper_re.shape[2]
    inverse_re = [None] * size
    inverse_im = [None] * size
    for across in range(size - 1, -1, -1):
        accum_re = jnp.broadcast_to(jnp.where(column_ids == across, 1.0, 0.0), (size, lines)).astype(jnp.float32)
        accum_im = jnp.zeros((size, lines), jnp.float32)
        if across < size - 1:
            later_re = jnp.stack(inverse_re[across + 1:])
            later_im = jnp.stack(inverse_im[across + 1:])
            coef_re = upper_re[across, across + 1:, :][:, None, :]
            coef_im = upper_im[across, across + 1:, :][:, None, :]
            accum_re = accum_re - lax.optimization_barrier(jnp.sum(coef_re * later_re - coef_im * later_im, axis=0))
            accum_im = accum_im - lax.optimization_barrier(jnp.sum(coef_re * later_im + coef_im * later_re, axis=0))
        pivot_value = upper_re[across, across][None, :]
        inverse_re[across] = accum_re / pivot_value
        inverse_im[across] = accum_im / pivot_value
    return (jnp.stack(inverse_re), jnp.stack(inverse_im))

def spectra_of(rows, table):
    count = rows.shape[0]
    flat_rows = rows.reshape(count * SEGMENTS, SEG_LEN).astype(jnp.float32)
    both = jnp.dot(flat_rows, table.astype(jnp.float32), precision=lax.Precision.HIGHEST)
    both = both.reshape(count, SEGMENTS, 2, LINES)
    return (both[:, :, 0, :], both[:, :, 1, :])

def reference(strain, band_start, sketch_seed):
    table = dft_table(band_start, SEG_LEN, LINES)
    block_rows = math.gcd(CHANNELS, 1024)
    block_count = CHANNELS // block_rows
    strain_blocks = strain.reshape(block_count, block_rows, SAMPLES)
    block_starts = jnp.arange(block_count, dtype=jnp.int32) * block_rows
    scaling = 1.0 / (SEGMENTS * CHANNELS)
    zeros = jnp.zeros((SEGMENTS, SKETCH, LINES), jnp.float32)

    def sketch_step(totals, inputs):
        rows, start = inputs
        spec_re, spec_im = spectra_of(rows, table)
        sign_re, sign_im = sketch_signs(start, block_rows, sketch_seed, SKETCH)
        part_re, part_im = contract('csf,ck->skf', spec_re, spec_im, sign_re, sign_im, True)
        return ((totals[0] + part_re, totals[1] + part_im), None)
    (sketch_re, sketch_im), unused = lax.scan(sketch_step, (zeros, zeros), (strain_blocks, block_starts))

    def power_step(totals, rows):
        spec_re, spec_im = spectra_of(rows, table)
        first_re, first_im = contract('csf,skf->ckf', spec_re, spec_im, sketch_re, sketch_im, False)
        part_re, part_im = contract('csf,ckf->skf', spec_re, spec_im, first_re * scaling, first_im * scaling, True)
        return ((totals[0] + part_re, totals[1] + part_im), None)
    (power_re, power_im), unused = lax.scan(power_step, (zeros, zeros), strain_blocks)

    def range_block(rows):
        spec_re, spec_im = spectra_of(rows, table)
        basis_re, basis_im = contract('csf,skf->ckf', spec_re, spec_im, power_re, power_im, False)
        return (basis_re * scaling, basis_im * scaling)
    basis_re, basis_im = lax.map(range_block, strain_blocks)
    basis_re = basis_re.reshape(CHANNELS, SKETCH, LINES)
    basis_im = basis_im.reshape(CHANNELS, SKETCH, LINES)
    gram_re, gram_im = contract('cjf,ckf->jkf', basis_re, basis_im, basis_re, basis_im, True)
    factor_re, factor_im = cholesky_upper(gram_re, gram_im)
    inverse_re, inverse_im = upper_inverse(factor_re, factor_im)
    modes_re, modes_im = contract('cjf,jkf->ckf', basis_re, basis_im, inverse_re, inverse_im, False)
    root = math.sqrt(CHANNELS)
    modes = jnp.stack([modes_re * root, modes_im * root], axis=1)
    factor = jnp.stack([factor_re, factor_im], axis=0)
    return (modes, factor)
```

```python
import functools
import math

import jax
import jax.numpy as jnp
from jax import lax
from jax.experimental import pallas as pl
from jax.experimental.pallas import tpu as pltpu
from jax.sharding import PartitionSpec as P

SEGMENTS = 24
LINES = 128
SKETCH = 16
HALF_ROWS = SEGMENTS * 2 * SKETCH
MESH = pl.DeviceIdType.MESH


def dft_table(band_start, segment_length, line_count):
    times_idx = jnp.arange(segment_length, dtype=jnp.int32)[:, None]
    line_ids = band_start[0] + jnp.arange(line_count, dtype=jnp.int32)[None, :]
    residues = times_idx * line_ids % segment_length
    phases = 2.0 * math.pi / segment_length * residues.astype(jnp.float32)
    window = 0.5 - 0.5 * jnp.cos(2.0 * math.pi / segment_length * times_idx.astype(jnp.float32))
    weighting = window / math.sqrt(3.0 * segment_length / 8.0)
    return jnp.concatenate(
        [weighting * jnp.cos(phases), -weighting * jnp.sin(phases)], axis=1
    ).astype(jnp.bfloat16)


def sign_block(first_channel, seed, channels, copies):
    shape = (2 * SKETCH, copies * channels)
    row = lax.broadcasted_iota(jnp.int32, shape, 0)
    col = lax.broadcasted_iota(jnp.int32, shape, 1)
    channel = first_channel + jnp.bitwise_and(col, channels - 1)
    half = (row >= SKETCH).astype(jnp.int32)
    column = row - half * SKETCH
    hashed = (channel * SKETCH + column) * 2 + half + seed * 1000003
    hashed = hashed * -1640531535
    hashed = jnp.bitwise_xor(hashed, lax.shift_right_logical(hashed, jnp.full_like(hashed, 15)))
    hashed = hashed * 2146121005
    hashed = jnp.bitwise_xor(hashed, lax.shift_right_logical(hashed, jnp.full_like(hashed, 13)))
    bits = jnp.bitwise_and(lax.shift_right_logical(hashed, jnp.full_like(hashed, 7)), 1)
    return (1 - 2 * bits).astype(jnp.float32)


def gram_row(t, s, part):
    block = t // 8
    return 8 * (0, 16, 48)[block] + (t % 8) * 16 * (block + 1) + part * 8 * (block + 1) + s


def sum_kernel(dims, strain, table, seed, full_out, sre, sim,
               part, crecv, xrecv, zflat, zbuf, zrecv, zgat, full,
               c_send, c_recv, x_send, x_recv, z_send, z_recv, g_send, g_recv, a_send, a_recv, f_send, f_recv):
    nx, ny, nz = dims
    planes = nx * ny
    rows = HALF_ROWS // planes
    zrows = rows // nz
    channels = strain.shape[0]
    length = table.shape[0]

    me = lax.axis_index("ch")
    core = lax.rem(me, 2)
    z = lax.rem(lax.div(me, 2), nz)
    p = lax.div(me, 2 * nz)
    x, y = lax.div(p, ny), lax.rem(p, ny)
    mate = me + 1 - 2 * core

    def plane_at(d, sign):
        dx, dy = d // ny, d % ny
        qx = lax.rem(x + (dx if sign > 0 else nx - dx), nx)
        qy = lax.rem(y + (dy if sign > 0 else ny - dy), ny)
        return qx * ny + qy

    def plane_device(q):
        return q * (2 * nz) + z * 2 + core

    def z_at(d):
        return lax.rem(z + d, nz)

    def z_device(k):
        return p * (2 * nz) + k * 2 + core

    barrier = pltpu.get_barrier_semaphore()
    pl.semaphore_signal(barrier, inc=1, device_id=(mate,), device_id_type=MESH)
    for d in range(1, planes):
        pl.semaphore_signal(barrier, inc=1, device_id=(plane_device(plane_at(d, 1)),), device_id_type=MESH)
    for d in range(1, nz):
        pl.semaphore_signal(barrier, inc=1, device_id=(z_device(z_at(d)),), device_id_type=MESH)

    for s in range(SEGMENTS):
        both = jnp.dot(strain[:, s * length:(s + 1) * length], table[...], preferred_element_type=jnp.float32)
        sre[s * channels:(s + 1) * channels, :] = both[:, :LINES]
        sim[s * channels:(s + 1) * channels, :] = both[:, LINES:]

    signs = sign_block(me * channels, seed[0], channels, 3).astype(jnp.bfloat16)
    for s in range(SEGMENTS):
        both = jnp.concatenate([sre[s * channels:(s + 1) * channels, :], sim[s * channels:(s + 1) * channels, :]], axis=1)
        high = both.astype(jnp.bfloat16)
        rest = both - high.astype(jnp.float32)
        middle = rest.astype(jnp.bfloat16)
        low = (rest - middle.astype(jnp.float32)).astype(jnp.bfloat16)
        terms = jnp.concatenate([high, middle, low], axis=0)
        prod = jnp.dot(signs, terms, preferred_element_type=jnp.float32)
        for half, value in enumerate((
            prod[:SKETCH, :LINES] + prod[SKETCH:, LINES:],
            prod[SKETCH:, :LINES] - prod[:SKETCH, LINES:],
        )):
            row = s * 2 * SKETCH + half * SKETCH
            part[0, row // rows, row % rows:row % rows + SKETCH, :] = value

    for t0 in range(0, SEGMENTS, 4):
        n = 8 * (t0 // 8 + 1)

        def step(i, accs, t0=t0, n=n):
            accs = list(accs)
            for k in range(4):
                c = i * 4 + k
                vre = sre[pl.ds(c, n, stride=channels), :]
                vim = sim[pl.ds(c, n, stride=channels), :]
                for a in range(4):
                    bre = sre[pl.ds((t0 + a) * channels + c, 1), :]
                    bim = sim[pl.ds((t0 + a) * channels + c, 1), :]
                    accs[2 * a] += vre * bre + vim * bim
                    accs[2 * a + 1] += vre * bim - vim * bre
            return tuple(accs)

        zero = jnp.zeros((n, LINES), jnp.float32)
        accs = lax.fori_loop(0, channels // 4, step, (zero,) * 8)
        for a in range(4):
            for half in range(2):
                for tile in range(n // 8):
                    row = gram_row(t0 + a, 8 * tile, half)
                    part[1, row // rows, row % rows:row % rows + 8, :] = accs[2 * a + half][8 * tile:8 * tile + 8, :]

    pl.semaphore_wait(barrier, planes + nz - 1)

    def remote(src, dst, send, recv, device):
        return pltpu.make_async_remote_copy(
            src_ref=src, dst_ref=dst, send_sem=send, recv_sem=recv, device_id=(device,), device_id_type=MESH
        )

    sends = []
    order = list(range(1, planes)) + [0]
    pair = {}
    for d in order:
        q = plane_at(d, 1)
        pair[d] = remote(part.at[1 - core, q], crecv.at[q], c_send.at[d], c_recv.at[d], mate)
        pair[d].start()
    for d in order:
        q = plane_at(d, 1)
        pair[d].wait_recv()
        crecv[q] = crecv[q] + part[core, q]
        if d:
            copy = remote(crecv.at[q], xrecv.at[d], x_send.at[d], x_recv.at[d], plane_device(q))
            copy.start()
            sends.append(copy)
    total = crecv[p]
    for d in range(1, planes):
        sends[d - 1].wait_recv()
        total = total + xrecv[d]
    zflat[...] = total
    for k in range(nz):
        zbuf[k] = zflat[k * zrows:(k + 1) * zrows, :]
    zcopies = []
    for d in range(1, nz):
        k = z_at(d)
        copy = remote(zbuf.at[k], zrecv.at[d], z_send.at[d], z_recv.at[d], z_device(k))
        copy.start()
        zcopies.append(copy)
    mine = zbuf[z]
    for d in range(1, nz):
        zcopies[d - 1].wait_recv()
        mine = mine + zrecv[d]
    zgat[z] = mine
    gcopies = []
    for d in range(1, nz):
        copy = remote(zgat.at[z], zgat.at[z], g_send.at[d], g_recv.at[d], z_device(z_at(d)))
        copy.start()
        gcopies.append(copy)
    for copy in gcopies:
        copy.wait_recv()
    for k in range(nz):
        full[core, p, k * zrows:(k + 1) * zrows, :] = zgat[k]
    acopies = []
    for d in range(1, planes):
        copy = remote(full.at[core, p], full.at[core, p], a_send.at[d], a_recv.at[d], plane_device(plane_at(d, 1)))
        copy.start()
        acopies.append(copy)
    fcopies = []
    for d in range(planes):
        q = plane_at(d, -1)
        if d:
            acopies[d - 1].wait_recv()
        copy = remote(full.at[core, q], full.at[core, q], f_send.at[d], f_recv.at[d], mate)
        copy.start()
        fcopies.append(copy)
    for copy in fcopies:
        copy.wait_recv()
    for copy in [pair[d] for d in order] + sends + zcopies + gcopies + acopies + fcopies:
        copy.wait_send()
    full_out[...] = full[...]


def all_sums(dims, strain, table, seed):
    nx, ny, nz = dims
    planes = nx * ny
    rows = HALF_ROWS // planes
    channels = strain.shape[0]
    vmem = pl.BlockSpec(memory_space=pltpu.VMEM)
    dma = pltpu.SemaphoreType.DMA
    spectrum = jax.ShapeDtypeStruct((SEGMENTS * channels, LINES), jnp.float32)
    return pl.pallas_call(
        functools.partial(sum_kernel, dims),
        out_shape=[jax.ShapeDtypeStruct((2, planes, rows, LINES), jnp.float32), spectrum, spectrum],
        in_specs=[vmem, vmem, pl.BlockSpec(memory_space=pltpu.SMEM)],
        out_specs=[vmem, vmem, vmem],
        scratch_shapes=[
            pltpu.VMEM((2, planes, rows, LINES), jnp.float32),
            pltpu.VMEM((planes, rows, LINES), jnp.float32),
            pltpu.VMEM((planes, rows, LINES), jnp.float32),
            pltpu.VMEM((rows, LINES), jnp.float32),
            pltpu.VMEM((nz, rows // nz, LINES), jnp.float32),
            pltpu.VMEM((nz, rows // nz, LINES), jnp.float32),
            pltpu.VMEM((nz, rows // nz, LINES), jnp.float32),
            pltpu.VMEM((2, planes, rows, LINES), jnp.float32),
        ] + [dma((planes,))] * 4 + [dma((nz,))] * 4 + [dma((planes,))] * 4,
        compiler_params=pltpu.CompilerParams(
            collective_id=0, has_side_effects=True, vmem_limit_bytes=48 * 1024 * 1024
        ),
        name="sums",
    )(strain, table, seed)


def mode_kernel(scaling, root, full, sre, sim, modes, factor, sky, px, py, hx, hy, gram, rows_x, basis):
    channels = sre.shape[0] // SEGMENTS

    def turned(value):
        return jnp.stack([-value[1], value[0]])

    def sketch_of(t):
        row = t * 2 * SKETCH
        return jnp.stack([full[0, row:row + SKETCH, :], full[0, row + SKETCH:row + 2 * SKETCH, :]])

    def gram_of(s, t):
        if s // 8 <= t // 8:
            first, second, sign = t, s, 1
        else:
            first, second, sign = s, t, -1
        row = gram_row(first, second, 0)
        row_im = gram_row(first, second, 1)
        return full[1, row:row + 1, :], full[1, row_im:row_im + 1, :], sign

    for t in range(SEGMENTS):
        sky[t] = turned(sketch_of(t))

    def times_gram(get_x, get_y, out_x, out_y, scale):
        for s0 in range(0, SEGMENTS, 4):
            accs = [jnp.zeros((2, SKETCH, LINES), jnp.float32) for _ in range(4)]
            for t in range(SEGMENTS):
                vx, vy = get_x(t), get_y(t)
                for a in range(4):
                    gre, gim, sign = gram_of(s0 + a, t)
                    if sign > 0:
                        accs[a] = accs[a] + gre * vx + gim * vy
                    else:
                        accs[a] = accs[a] + gre * vx - gim * vy
            for a in range(4):
                value = accs[a] if scale is None else accs[a] * scale * scale
                out_x[s0 + a] = value
                out_y[s0 + a] = turned(value)

    times_gram(sketch_of, lambda t: sky[t], px, py, scaling)
    times_gram(lambda t: px[t], lambda t: py[t], hx, hy, None)

    for j0 in range(0, SKETCH, 4):
        k0 = 8 * (j0 // 8)
        accs = [jnp.zeros((2, SKETCH - k0, LINES), jnp.float32) for _ in range(4)]
        for s in range(SEGMENTS):
            vx, vy = hx[s, :, k0:, :], hy[s, :, k0:, :]
            for a in range(4):
                accs[a] = accs[a] + px[s, 0, j0 + a:j0 + a + 1, :] * vx - px[s, 1, j0 + a:j0 + a + 1, :] * vy
        for a in range(4):
            gram[j0 + a, :, k0:, :] = accs[a]

    for j0 in range(0, SKETCH, 4):
        accs = [jnp.zeros((2, channels, LINES), jnp.float32) for _ in range(4)]
        for s in range(SEGMENTS):
            vx = jnp.stack([sre[s * channels:(s + 1) * channels, :], sim[s * channels:(s + 1) * channels, :]])
            vy = turned(vx)
            for a in range(4):
                accs[a] = accs[a] + px[s, 0, j0 + a:j0 + a + 1, :] * vx + px[s, 1, j0 + a:j0 + a + 1, :] * vy
        for a in range(4):
            basis[j0 + a] = accs[a]

    for i in range(SKETCH):
        k0 = 8 * (i // 8)
        columns = k0 + lax.broadcasted_iota(jnp.int32, (SKETCH - k0, LINES), 0)
        row = gram[i, :, k0:, :]
        diagonal = jnp.sqrt(gram[i, 0, i:i + 1, :])
        inverse = 1.0 / diagonal
        scaled = row * inverse
        re = jnp.where(columns > i, scaled[0], 0.0)
        re = jnp.where(columns == i, diagonal, re)
        im = jnp.where(columns > i, scaled[1], 0.0)
        value = jnp.stack([re, im])
        if k0:
            factor[0, i, :k0, :] = jnp.zeros((k0, LINES), jnp.float32)
            factor[1, i, :k0, :] = jnp.zeros((k0, LINES), jnp.float32)
        factor[0, i, k0:, :] = re
        factor[1, i, k0:, :] = im
        rows_x[i, :, k0:, :] = value
        mode = basis[i] * inverse
        modes[pl.ds(i, channels, stride=2 * SKETCH), :] = mode[0] * root
        modes[pl.ds(i + SKETCH, channels, stride=2 * SKETCH), :] = mode[1] * root
        other = turned(mode)
        for r in range(i + 1, SKETCH):
            r0 = 8 * (r // 8)
            top_re = rows_x[i, 0, r:r + 1, :]
            top_im = rows_x[i, 1, r:r + 1, :]
            late = value[:, r0 - k0:, :]
            gram[r, :, r0:, :] = gram[r, :, r0:, :] - (top_re * late - top_im * turned(late))
            basis[r] = basis[r] - (top_re * mode + top_im * other)


def finish(full, sre, sim, channels_all):
    channels = sre.shape[0] // SEGMENTS
    vmem = pl.BlockSpec(memory_space=pltpu.VMEM)
    kernel = functools.partial(mode_kernel, 1.0 / (SEGMENTS * channels_all), math.sqrt(channels_all))
    tall = pltpu.VMEM((SEGMENTS, 2, SKETCH, LINES), jnp.float32)
    wide = pltpu.VMEM((SKETCH, 2, SKETCH, LINES), jnp.float32)
    return pl.pallas_call(
        kernel,
        out_shape=[
            jax.ShapeDtypeStruct((channels * 2 * SKETCH, LINES), jnp.float32),
            jax.ShapeDtypeStruct((2, SKETCH, SKETCH, LINES), jnp.float32),
        ],
        in_specs=[vmem] * 3,
        out_specs=[vmem] * 2,
        scratch_shapes=[tall] * 5 + [wide] * 2 + [pltpu.VMEM((SKETCH, 2, channels, LINES), jnp.float32)],
        compiler_params=pltpu.CompilerParams(vmem_limit_bytes=48 * 1024 * 1024),
        name="modes",
    )(full, sre, sim)


def shards(dims, strain, band_start, sketch_seed):
    channels, samples = strain.shape
    channels_all = channels * lax.axis_size("ch")
    table = dft_table(band_start, samples // SEGMENTS, LINES)
    full, sre, sim = all_sums(dims, strain, table, sketch_seed)
    modes, factor = finish(full.reshape(2, HALF_ROWS, LINES), sre, sim, channels_all)
    return modes.reshape(channels, 2, SKETCH, LINES), factor


def solution(mesh, dims=(4, 4, 16)):
    in_specs = (P("ch", None), P(), P())
    out_specs = (P("ch", None, None, None), P())
    return jax.shard_map(
        functools.partial(shards, dims), mesh=mesh, in_specs=in_specs, out_specs=out_specs, check_vma=False
    )
```

```python
import functools
import math

import jax
import jax.numpy as jnp
from jax import lax
from jax.experimental import pallas as pl
from jax.experimental.pallas import tpu as pltpu
from jax.sharding import PartitionSpec as P

SEGMENTS = 24
LINES = 128
SKETCH = 16
HALF_ROWS = SEGMENTS * 2 * SKETCH
MESH = pl.DeviceIdType.MESH
GROUP = 4


def dft_table(band_start, segment_length, line_count):
    times_idx = jnp.arange(segment_length, dtype=jnp.int32)[:, None]
    line_ids = band_start[0] + jnp.arange(line_count, dtype=jnp.int32)[None, :]
    residues = times_idx * line_ids % segment_length
    phases = 2.0 * math.pi / segment_length * residues.astype(jnp.float32)
    window = 0.5 - 0.5 * jnp.cos(2.0 * math.pi / segment_length * times_idx.astype(jnp.float32))
    weighting = window / math.sqrt(3.0 * segment_length / 8.0)
    return jnp.concatenate(
        [weighting * jnp.cos(phases), -weighting * jnp.sin(phases)], axis=1
    ).astype(jnp.bfloat16)


def sign_block(first_channel, seed, channels, copies, group):
    shape = (group * 2 * SKETCH, group * copies * channels)
    row = lax.broadcasted_iota(jnp.int32, shape, 0)
    col = lax.broadcasted_iota(jnp.int32, shape, 1)
    inside = jnp.zeros(shape, jnp.bool_)
    for g in range(group):
        inside = inside | (
            (row >= g * 2 * SKETCH) & (row < (g + 1) * 2 * SKETCH)
            & (col >= g * copies * channels) & (col < (g + 1) * copies * channels)
        )
    channel = first_channel + jnp.bitwise_and(col, channels - 1)
    half = jnp.bitwise_and(lax.shift_right_logical(row, jnp.full_like(row, 4)), 1)
    column = jnp.bitwise_and(row, SKETCH - 1)
    hashed = (channel * SKETCH + column) * 2 + half + seed * 1000003
    hashed = hashed * -1640531535
    hashed = jnp.bitwise_xor(hashed, lax.shift_right_logical(hashed, jnp.full_like(hashed, 15)))
    hashed = hashed * 2146121005
    hashed = jnp.bitwise_xor(hashed, lax.shift_right_logical(hashed, jnp.full_like(hashed, 13)))
    bits = jnp.bitwise_and(lax.shift_right_logical(hashed, jnp.full_like(hashed, 7)), 1)
    return jnp.where(inside, (1 - 2 * bits).astype(jnp.float32), 0.0)


def gram_row(t, s, part):
    block = t // 8
    return 8 * (0, 16, 48)[block] + (t % 8) * 16 * (block + 1) + part * 8 * (block + 1) + s


def sum_kernel(dims, strain, table, seed, full_out, sre, sim,
               part, crecv, xrecv, zflat, zbuf, zrecv, zgat, full,
               c_send, c_recv, x_send, x_recv, z_send, z_recv, g_send, g_recv, a_send, a_recv, f_send, f_recv):
    nx, ny, nz = dims
    planes = nx * ny
    rows = HALF_ROWS // planes
    zrows = rows // nz
    channels = strain.shape[0]
    length = table.shape[0]

    me = lax.axis_index("ch")
    core = lax.rem(me, 2)
    z = lax.rem(lax.div(me, 2), nz)
    p = lax.div(me, 2 * nz)
    x, y = lax.div(p, ny), lax.rem(p, ny)
    mate = me + 1 - 2 * core

    def plane_at(d, sign):
        dx, dy = d // ny, d % ny
        qx = lax.rem(x + (dx if sign > 0 else nx - dx), nx)
        qy = lax.rem(y + (dy if sign > 0 else ny - dy), ny)
        return qx * ny + qy

    def plane_device(q):
        return q * (2 * nz) + z * 2 + core

    def z_at(d):
        return lax.rem(z + d, nz)

    def z_device(k):
        return p * (2 * nz) + k * 2 + core

    barrier = pltpu.get_barrier_semaphore()
    pl.semaphore_signal(barrier, inc=1, device_id=(mate,), device_id_type=MESH)
    for d in range(1, planes):
        pl.semaphore_signal(barrier, inc=1, device_id=(plane_device(plane_at(d, 1)),), device_id_type=MESH)
    for d in range(1, nz):
        pl.semaphore_signal(barrier, inc=1, device_id=(z_device(z_at(d)),), device_id_type=MESH)

    def remote(src, dst, send, recv, device):
        return pltpu.make_async_remote_copy(
            src_ref=src, dst_ref=dst, send_sem=send, recv_sem=recv, device_id=(device,), device_id_type=MESH
        )

    flat = jnp.concatenate([strain[:, s * length:(s + 1) * length] for s in range(SEGMENTS)], axis=0)
    both = jnp.dot(flat, table[...], preferred_element_type=jnp.float32)
    sre[...] = both[:, :LINES]
    sim[...] = both[:, LINES:]

    signs = sign_block(me * channels, seed[0], channels, 3, GROUP).astype(jnp.bfloat16)
    for s0 in range(0, SEGMENTS, GROUP):
        terms = []
        for s in range(s0, s0 + GROUP):
            both = jnp.concatenate(
                [sre[s * channels:(s + 1) * channels, :], sim[s * channels:(s + 1) * channels, :]], axis=1
            )
            high = both.astype(jnp.bfloat16)
            rest = both - high.astype(jnp.float32)
            middle = rest.astype(jnp.bfloat16)
            low = (rest - middle.astype(jnp.float32)).astype(jnp.bfloat16)
            terms += [high, middle, low]
        prods = jnp.dot(signs, jnp.concatenate(terms, axis=0), preferred_element_type=jnp.float32)
        for s in range(s0, s0 + GROUP):
            prod = prods[(s - s0) * 2 * SKETCH:(s - s0 + 1) * 2 * SKETCH, :]
            for half, value in enumerate((
                prod[:SKETCH, :LINES] + prod[SKETCH:, LINES:],
                prod[SKETCH:, :LINES] - prod[:SKETCH, LINES:],
            )):
                row = s * 2 * SKETCH + half * SKETCH
                part[0, row // rows, row % rows:row % rows + SKETCH, :] = value

    pl.semaphore_wait(barrier, planes + nz - 1)

    def pair(half, q):
        return remote(part.at[half, q], crecv.at[q], c_send.at[q], c_recv.at[q], mate)

    @pl.when(core == 1)
    def _():
        for q in range(planes):
            pair(0, q).start()

    def plane_copy(d):
        q = plane_at(d, 1)
        return remote(crecv.at[q], xrecv.at[d], x_send.at[d], x_recv.at[d], plane_device(q))

    def plane_sends():
        for d in list(range(1, planes)) + [0]:
            q = plane_at(d, 1)
            pair(core, q).wait_recv()
            crecv[q] = crecv[q] + part[core, q]
            if d:
                plane_copy(d).start()

    sent = planes
    for t0 in range(SEGMENTS - 4, -1, -4):
        n = 8 * (t0 // 8 + 1)
        zero = jnp.zeros((n, LINES), jnp.float32)
        accs = [zero] * 8
        for c in range(channels):
            vre = sre[pl.ds(c, n, stride=channels), :]
            vim = sim[pl.ds(c, n, stride=channels), :]
            for a in range(4):
                bre = sre[(t0 + a) * channels + c:(t0 + a) * channels + c + 1, :]
                bim = sim[(t0 + a) * channels + c:(t0 + a) * channels + c + 1, :]
                accs[2 * a] += vre * bre + vim * bim
                accs[2 * a + 1] += vre * bim - vim * bre
        for a in range(4):
            for half in range(2):
                for tile in range(n // 8):
                    row = gram_row(t0 + a, 8 * tile, half)
                    part[1, row // rows, row % rows:row % rows + 8, :] = accs[2 * a + half][8 * tile:8 * tile + 8, :]
        ready = [q for q in range(sent) if q * rows >= gram_row(t0, 0, 0)]
        sent -= len(ready)

        @pl.when(core == 0)
        def _(ready=ready, t0=t0):
            for q in ready:
                pair(1, q).start()
            if t0 == 8:
                plane_sends()

    @pl.when(core == 1)
    def _():
        plane_sends()

    sends = [plane_copy(d) for d in range(1, planes)]
    total = crecv[p]
    for d in range(1, planes):
        sends[d - 1].wait_recv()
        total = total + xrecv[d]
    zflat[...] = total
    for k in range(nz):
        zbuf[k] = zflat[k * zrows:(k + 1) * zrows, :]
    zcopies = []
    for d in range(1, nz):
        k = z_at(d)
        copy = remote(zbuf.at[k], zrecv.at[d], z_send.at[d], z_recv.at[d], z_device(k))
        copy.start()
        zcopies.append(copy)
    mine = zbuf[z]
    for d in range(1, nz):
        zcopies[d - 1].wait_recv()
        mine = mine + zrecv[d]
    zgat[z] = mine
    gcopies = []
    for d in range(1, nz):
        copy = remote(zgat.at[z], zgat.at[z], g_send.at[d], g_recv.at[d], z_device(z_at(d)))
        copy.start()
        gcopies.append(copy)
    for copy in gcopies:
        copy.wait_recv()
    for k in range(nz):
        full[core, p, k * zrows:(k + 1) * zrows, :] = zgat[k]
    acopies = []
    for d in range(1, planes):
        copy = remote(full.at[core, p], full.at[core, p], a_send.at[d], a_recv.at[d], plane_device(plane_at(d, 1)))
        copy.start()
        acopies.append(copy)
    fcopies = []
    for d in range(planes):
        q = plane_at(d, -1)
        if d:
            acopies[d - 1].wait_recv()
        copy = remote(full.at[core, q], full.at[core, q], f_send.at[d], f_recv.at[d], mate)
        copy.start()
        fcopies.append(copy)
    for copy in fcopies:
        copy.wait_recv()
    for copy in [pair(1 - core, q) for q in range(planes)] + sends + zcopies + gcopies + acopies + fcopies:
        copy.wait_send()
    full_out[...] = full[...]


def all_sums(dims, strain, table, seed):
    nx, ny, nz = dims
    planes = nx * ny
    rows = HALF_ROWS // planes
    channels = strain.shape[0]
    vmem = pl.BlockSpec(memory_space=pltpu.VMEM)
    dma = pltpu.SemaphoreType.DMA
    spectrum = jax.ShapeDtypeStruct((SEGMENTS * channels, LINES), jnp.float32)
    return pl.pallas_call(
        functools.partial(sum_kernel, dims),
        out_shape=[jax.ShapeDtypeStruct((2, planes, rows, LINES), jnp.float32), spectrum, spectrum],
        in_specs=[vmem, vmem, pl.BlockSpec(memory_space=pltpu.SMEM)],
        out_specs=[vmem, vmem, vmem],
        scratch_shapes=[
            pltpu.VMEM((2, planes, rows, LINES), jnp.float32),
            pltpu.VMEM((planes, rows, LINES), jnp.float32),
            pltpu.VMEM((planes, rows, LINES), jnp.float32),
            pltpu.VMEM((rows, LINES), jnp.float32),
            pltpu.VMEM((nz, rows // nz, LINES), jnp.float32),
            pltpu.VMEM((nz, rows // nz, LINES), jnp.float32),
            pltpu.VMEM((nz, rows // nz, LINES), jnp.float32),
            pltpu.VMEM((2, planes, rows, LINES), jnp.float32),
        ] + [dma((planes,))] * 4 + [dma((nz,))] * 4 + [dma((planes,))] * 4,
        compiler_params=pltpu.CompilerParams(
            collective_id=0, has_side_effects=True, vmem_limit_bytes=48 * 1024 * 1024
        ),
        name="sums",
    )(strain, table, seed)


def mode_kernel(scaling, root, full, sre, sim, modes, factor, sky, px, py, hx, hy, gram, rows_x, basis):
    channels = sre.shape[0] // SEGMENTS

    def turned(value):
        return jnp.stack([-value[1], value[0]])

    def sketch_of(t):
        row = t * 2 * SKETCH
        return jnp.stack([full[0, row:row + SKETCH, :], full[0, row + SKETCH:row + 2 * SKETCH, :]])

    def gram_of(s, t):
        if s // 8 <= t // 8:
            first, second, sign = t, s, 1
        else:
            first, second, sign = s, t, -1
        row = gram_row(first, second, 0)
        row_im = gram_row(first, second, 1)
        return full[1, row:row + 1, :], full[1, row_im:row_im + 1, :], sign

    for t in range(SEGMENTS):
        sky[t] = turned(sketch_of(t))

    def times_gram(get_x, get_y, out_x, out_y, scale):
        for s0 in range(0, SEGMENTS, 4):
            accs = [jnp.zeros((2, SKETCH, LINES), jnp.float32) for _ in range(4)]
            for t in range(SEGMENTS):
                vx, vy = get_x(t), get_y(t)
                for a in range(4):
                    gre, gim, sign = gram_of(s0 + a, t)
                    if sign > 0:
                        accs[a] = accs[a] + gre * vx + gim * vy
                    else:
                        accs[a] = accs[a] + gre * vx - gim * vy
            for a in range(4):
                value = accs[a] if scale is None else accs[a] * scale * scale
                out_x[s0 + a] = value
                out_y[s0 + a] = turned(value)

    times_gram(sketch_of, lambda t: sky[t], px, py, scaling)
    times_gram(lambda t: px[t], lambda t: py[t], hx, hy, None)

    for j0 in range(0, SKETCH, 4):
        k0 = 8 * (j0 // 8)
        accs = [jnp.zeros((2, SKETCH - k0, LINES), jnp.float32) for _ in range(4)]
        for s in range(SEGMENTS):
            vx, vy = hx[s, :, k0:, :], hy[s, :, k0:, :]
            for a in range(4):
                accs[a] = accs[a] + px[s, 0, j0 + a:j0 + a + 1, :] * vx - px[s, 1, j0 + a:j0 + a + 1, :] * vy
        for a in range(4):
            gram[j0 + a, :, k0:, :] = accs[a]

    for j0 in range(0, SKETCH, 4):
        accs = [jnp.zeros((2, channels, LINES), jnp.float32) for _ in range(4)]
        for s in range(SEGMENTS):
            vx = jnp.stack([sre[s * channels:(s + 1) * channels, :], sim[s * channels:(s + 1) * channels, :]])
            vy = turned(vx)
            for a in range(4):
                accs[a] = accs[a] + px[s, 0, j0 + a:j0 + a + 1, :] * vx + px[s, 1, j0 + a:j0 + a + 1, :] * vy
        for a in range(4):
            basis[j0 + a] = accs[a]

    for i in range(SKETCH):
        k0 = 8 * (i // 8)
        columns = k0 + lax.broadcasted_iota(jnp.int32, (SKETCH - k0, LINES), 0)
        row = gram[i, :, k0:, :]
        diagonal = jnp.sqrt(gram[i, 0, i:i + 1, :])
        inverse = 1.0 / diagonal
        scaled = row * inverse
        re = jnp.where(columns > i, scaled[0], 0.0)
        re = jnp.where(columns == i, diagonal, re)
        im = jnp.where(columns > i, scaled[1], 0.0)
        value = jnp.stack([re, im])
        if k0:
            factor[0, i, :k0, :] = jnp.zeros((k0, LINES), jnp.float32)
            factor[1, i, :k0, :] = jnp.zeros((k0, LINES), jnp.float32)
        factor[0, i, k0:, :] = re
        factor[1, i, k0:, :] = im
        rows_x[i, :, k0:, :] = value
        mode = basis[i] * inverse
        modes[pl.ds(i, channels, stride=2 * SKETCH), :] = mode[0] * root
        modes[pl.ds(i + SKETCH, channels, stride=2 * SKETCH), :] = mode[1] * root
        other = turned(mode)
        for r in range(i + 1, SKETCH):
            r0 = 8 * (r // 8)
            top_re = rows_x[i, 0, r:r + 1, :]
            top_im = rows_x[i, 1, r:r + 1, :]
            late = value[:, r0 - k0:, :]
            gram[r, :, r0:, :] = gram[r, :, r0:, :] - (top_re * late - top_im * turned(late))
            basis[r] = basis[r] - (top_re * mode + top_im * other)


def finish(full, sre, sim, channels_all):
    channels = sre.shape[0] // SEGMENTS
    vmem = pl.BlockSpec(memory_space=pltpu.VMEM)
    kernel = functools.partial(mode_kernel, 1.0 / (SEGMENTS * channels_all), math.sqrt(channels_all))
    tall = pltpu.VMEM((SEGMENTS, 2, SKETCH, LINES), jnp.float32)
    wide = pltpu.VMEM((SKETCH, 2, SKETCH, LINES), jnp.float32)
    return pl.pallas_call(
        kernel,
        out_shape=[
            jax.ShapeDtypeStruct((channels * 2 * SKETCH, LINES), jnp.float32),
            jax.ShapeDtypeStruct((2, SKETCH, SKETCH, LINES), jnp.float32),
        ],
        in_specs=[vmem] * 3,
        out_specs=[vmem] * 2,
        scratch_shapes=[tall] * 5 + [wide] * 2 + [pltpu.VMEM((SKETCH, 2, channels, LINES), jnp.float32)],
        compiler_params=pltpu.CompilerParams(vmem_limit_bytes=48 * 1024 * 1024),
        name="modes",
    )(full, sre, sim)


def shards(dims, strain, band_start, sketch_seed):
    channels, samples = strain.shape
    channels_all = channels * lax.axis_size("ch")
    table = dft_table(band_start, samples // SEGMENTS, LINES)
    full, sre, sim = all_sums(dims, strain, table, sketch_seed)
    modes, factor = finish(full.reshape(2, HALF_ROWS, LINES), sre, sim, channels_all)
    return modes.reshape(channels, 2, SKETCH, LINES), factor


def solution(mesh, dims=(4, 4, 16)):
    in_specs = (P("ch", None), P(), P())
    out_specs = (P("ch", None, None, None), P())
    return jax.shard_map(
        functools.partial(shards, dims), mesh=mesh, in_specs=in_specs, out_specs=out_specs, check_vma=False
    )
```

```python
import functools
import math

import jax
import jax.numpy as jnp
from jax import lax
from jax.experimental import pallas as pl
from jax.experimental.pallas import tpu as pltpu
from jax.sharding import PartitionSpec as P

SEGMENTS = 24
LINES = 128
SKETCH = 16
HALF_ROWS = SEGMENTS * 2 * SKETCH
MESH = pl.DeviceIdType.MESH
GROUP = 4


def dft_table(band_start, segment_length, line_count):
    times_idx = jnp.arange(segment_length, dtype=jnp.int32)[:, None]
    line_ids = band_start[0] + jnp.arange(line_count, dtype=jnp.int32)[None, :]
    residues = times_idx * line_ids % segment_length
    phases = 2.0 * math.pi / segment_length * residues.astype(jnp.float32)
    window = 0.5 - 0.5 * jnp.cos(2.0 * math.pi / segment_length * times_idx.astype(jnp.float32))
    weighting = window / math.sqrt(3.0 * segment_length / 8.0)
    return jnp.concatenate(
        [weighting * jnp.cos(phases), -weighting * jnp.sin(phases)], axis=1
    ).astype(jnp.bfloat16)


def sign_block(first_channel, seed, channels, copies, group):
    shape = (group * 2 * SKETCH, group * copies * channels)
    row = lax.broadcasted_iota(jnp.int32, shape, 0)
    col = lax.broadcasted_iota(jnp.int32, shape, 1)
    inside = jnp.zeros(shape, jnp.bool_)
    for g in range(group):
        inside = inside | (
            (row >= g * 2 * SKETCH) & (row < (g + 1) * 2 * SKETCH)
            & (col >= g * copies * channels) & (col < (g + 1) * copies * channels)
        )
    channel = first_channel + jnp.bitwise_and(col, channels - 1)
    half = jnp.bitwise_and(lax.shift_right_logical(row, jnp.full_like(row, 4)), 1)
    column = jnp.bitwise_and(row, SKETCH - 1)
    hashed = (channel * SKETCH + column) * 2 + half + seed * 1000003
    hashed = hashed * -1640531535
    hashed = jnp.bitwise_xor(hashed, lax.shift_right_logical(hashed, jnp.full_like(hashed, 15)))
    hashed = hashed * 2146121005
    hashed = jnp.bitwise_xor(hashed, lax.shift_right_logical(hashed, jnp.full_like(hashed, 13)))
    bits = jnp.bitwise_and(lax.shift_right_logical(hashed, jnp.full_like(hashed, 7)), 1)
    return jnp.where(inside, (1 - 2 * bits).astype(jnp.float32), 0.0)


def gram_row(t, s, part):
    block = t // 8
    return 8 * (0, 16, 48)[block] + (t % 8) * 16 * (block + 1) + part * 8 * (block + 1) + s


def sum_kernel(dims, strain, table, seed, full_out, sre, sim,
               part, crecv, xrecv, zflat, zbuf, zrecv, zgat, full,
               c_send, c_recv, x_send, x_recv, z_send, z_recv, g_send, g_recv, a_send, a_recv, f_send, f_recv):
    nx, ny, nz = dims
    planes = nx * ny
    rows = HALF_ROWS // planes
    zrows = rows // nz
    channels = strain.shape[0]
    length = table.shape[0]

    me = lax.axis_index("ch")
    core = lax.rem(me, 2)
    z = lax.rem(lax.div(me, 2), nz)
    p = lax.div(me, 2 * nz)
    x, y = lax.div(p, ny), lax.rem(p, ny)
    mate = me + 1 - 2 * core

    def plane_at(d, sign):
        dx, dy = d // ny, d % ny
        qx = lax.rem(x + (dx if sign > 0 else nx - dx), nx)
        qy = lax.rem(y + (dy if sign > 0 else ny - dy), ny)
        return qx * ny + qy

    def plane_device(q):
        return q * (2 * nz) + z * 2 + core

    def z_at(d):
        return lax.rem(z + d, nz)

    def z_device(k):
        return p * (2 * nz) + k * 2 + core

    barrier = pltpu.get_barrier_semaphore()
    pl.semaphore_signal(barrier, inc=1, device_id=(mate,), device_id_type=MESH)
    for d in range(1, planes):
        pl.semaphore_signal(barrier, inc=1, device_id=(plane_device(plane_at(d, 1)),), device_id_type=MESH)
    for d in range(1, nz):
        pl.semaphore_signal(barrier, inc=1, device_id=(z_device(z_at(d)),), device_id_type=MESH)

    def remote(src, dst, send, recv, device):
        return pltpu.make_async_remote_copy(
            src_ref=src, dst_ref=dst, send_sem=send, recv_sem=recv, device_id=(device,), device_id_type=MESH
        )

    flat = jnp.concatenate([strain[:, s * length:(s + 1) * length] for s in range(SEGMENTS)], axis=0)
    both = jnp.dot(flat, table[...], preferred_element_type=jnp.float32)
    sre[...] = both[:, :LINES]
    sim[...] = both[:, LINES:]

    signs = sign_block(me * channels, seed[0], channels, 3, GROUP).astype(jnp.bfloat16)
    for s0 in range(0, SEGMENTS, GROUP):
        terms = []
        for s in range(s0, s0 + GROUP):
            both = jnp.concatenate(
                [sre[s * channels:(s + 1) * channels, :], sim[s * channels:(s + 1) * channels, :]], axis=1
            )
            high = both.astype(jnp.bfloat16)
            rest = both - high.astype(jnp.float32)
            middle = rest.astype(jnp.bfloat16)
            low = (rest - middle.astype(jnp.float32)).astype(jnp.bfloat16)
            terms += [high, middle, low]
        prods = jnp.dot(signs, jnp.concatenate(terms, axis=0), preferred_element_type=jnp.float32)
        for s in range(s0, s0 + GROUP):
            prod = prods[(s - s0) * 2 * SKETCH:(s - s0 + 1) * 2 * SKETCH, :]
            for half, value in enumerate((
                prod[:SKETCH, :LINES] + prod[SKETCH:, LINES:],
                prod[SKETCH:, :LINES] - prod[:SKETCH, LINES:],
            )):
                row = s * 2 * SKETCH + half * SKETCH
                part[0, row // rows, row % rows:row % rows + SKETCH, :] = value

    pl.semaphore_wait(barrier, planes + nz - 1)

    def landed(ref, sem):
        pltpu.make_async_copy(ref, ref, sem).wait()

    def pair(half, q, count):
        span = pl.ds(q, count)
        return remote(part.at[half, span], crecv.at[span], c_send, c_recv, mate)

    @pl.when(core == 1)
    def _():
        pair(0, 0, planes).start()

    sent = planes
    for t0 in range(SEGMENTS - 4, -1, -4):
        n = 8 * (t0 // 8 + 1)
        zero = jnp.zeros((n, LINES), jnp.float32)
        accs = [zero] * 8
        for c in range(channels):
            vre = sre[pl.ds(c, n, stride=channels), :]
            vim = sim[pl.ds(c, n, stride=channels), :]
            for a in range(4):
                bre = sre[(t0 + a) * channels + c:(t0 + a) * channels + c + 1, :]
                bim = sim[(t0 + a) * channels + c:(t0 + a) * channels + c + 1, :]
                accs[2 * a] += vre * bre + vim * bim
                accs[2 * a + 1] += vre * bim - vim * bre
        for a in range(4):
            for half in range(2):
                for tile in range(n // 8):
                    row = gram_row(t0 + a, 8 * tile, half)
                    part[1, row // rows, row % rows:row % rows + 8, :] = accs[2 * a + half][8 * tile:8 * tile + 8, :]
        first = -(-gram_row(t0, 0, 0) // rows)

        if first < sent:
            @pl.when(core == 0)
            def _(first=first, count=sent - first):
                pair(1, first, count).start()
        sent = min(sent, first)

    landed(crecv, c_recv)
    for d in range(1, planes):
        q = plane_at(d, 1)
        crecv[q] = crecv[q] + part[core, q]
        remote(crecv.at[q], xrecv.at[d], x_send, x_recv, plane_device(q)).start()
    total = crecv[p] + part[core, p]
    landed(xrecv.at[pl.ds(1, planes - 1)], x_recv)
    for d in range(1, planes):
        total = total + xrecv[d]
    zflat[...] = total
    for k in range(nz):
        zbuf[k] = zflat[k * zrows:(k + 1) * zrows, :]
    zcopies = []
    for d in range(1, nz):
        k = z_at(d)
        copy = remote(zbuf.at[k], zrecv.at[d], z_send.at[d], z_recv.at[d], z_device(k))
        copy.start()
        zcopies.append(copy)
    mine = zbuf[z]
    for d in range(1, nz):
        zcopies[d - 1].wait_recv()
        mine = mine + zrecv[d]
    zgat[z] = mine
    gcopies = []
    for d in range(1, nz):
        copy = remote(zgat.at[z], zgat.at[z], g_send.at[d], g_recv.at[d], z_device(z_at(d)))
        copy.start()
        gcopies.append(copy)
    for copy in gcopies:
        copy.wait_recv()
    for k in range(nz):
        full[core, p, k * zrows:(k + 1) * zrows, :] = zgat[k]
    acopies = []
    for d in range(1, planes):
        copy = remote(full.at[core, p], full.at[core, p], a_send, a_recv.at[d], plane_device(plane_at(d, 1)))
        copy.start()
        acopies.append(copy)
    for d in range(planes):
        q = plane_at(d, -1)
        if d:
            acopies[d - 1].wait_recv()
        remote(full.at[core, q], full.at[core, q], f_send, f_recv, mate).start()
    landed(full.at[1 - core], f_recv)
    landed(full.at[core], f_send)
    landed(crecv, c_send)
    landed(xrecv.at[pl.ds(1, planes - 1)], x_send)
    landed(xrecv.at[pl.ds(1, planes - 1)], a_send)
    for copy in zcopies + gcopies:
        copy.wait_send()
    full_out[...] = full[...]


def all_sums(dims, strain, table, seed):
    nx, ny, nz = dims
    planes = nx * ny
    rows = HALF_ROWS // planes
    channels = strain.shape[0]
    vmem = pl.BlockSpec(memory_space=pltpu.VMEM)
    dma = pltpu.SemaphoreType.DMA
    spectrum = jax.ShapeDtypeStruct((SEGMENTS * channels, LINES), jnp.float32)
    return pl.pallas_call(
        functools.partial(sum_kernel, dims),
        out_shape=[jax.ShapeDtypeStruct((2, planes, rows, LINES), jnp.float32), spectrum, spectrum],
        in_specs=[vmem, vmem, pl.BlockSpec(memory_space=pltpu.SMEM)],
        out_specs=[vmem, vmem, vmem],
        scratch_shapes=[
            pltpu.VMEM((2, planes, rows, LINES), jnp.float32),
            pltpu.VMEM((planes, rows, LINES), jnp.float32),
            pltpu.VMEM((planes, rows, LINES), jnp.float32),
            pltpu.VMEM((rows, LINES), jnp.float32),
            pltpu.VMEM((nz, rows // nz, LINES), jnp.float32),
            pltpu.VMEM((nz, rows // nz, LINES), jnp.float32),
            pltpu.VMEM((nz, rows // nz, LINES), jnp.float32),
            pltpu.VMEM((2, planes, rows, LINES), jnp.float32),
        ] + [dma(())] * 4 + [dma((nz,))] * 4 + [dma(()), dma((planes,)), dma(()), dma(())],
        compiler_params=pltpu.CompilerParams(
            collective_id=0, has_side_effects=True, vmem_limit_bytes=48 * 1024 * 1024
        ),
        name="sums",
    )(strain, table, seed)


def mode_kernel(scaling, root, full, sre, sim, modes, factor, sky, px, py, hx, hy, gram, rows_x, basis):
    channels = sre.shape[0] // SEGMENTS

    def turned(value):
        return jnp.stack([-value[1], value[0]])

    def sketch_of(t):
        row = t * 2 * SKETCH
        return jnp.stack([full[0, row:row + SKETCH, :], full[0, row + SKETCH:row + 2 * SKETCH, :]])

    def gram_of(s, t):
        if s // 8 <= t // 8:
            first, second, sign = t, s, 1
        else:
            first, second, sign = s, t, -1
        row = gram_row(first, second, 0)
        row_im = gram_row(first, second, 1)
        return full[1, row:row + 1, :], full[1, row_im:row_im + 1, :], sign

    for t in range(SEGMENTS):
        sky[t] = turned(sketch_of(t))

    def times_gram(get_x, get_y, out_x, out_y, scale):
        for s0 in range(0, SEGMENTS, 4):
            accs = [jnp.zeros((2, SKETCH, LINES), jnp.float32) for _ in range(4)]
            for t in range(SEGMENTS):
                vx, vy = get_x(t), get_y(t)
                for a in range(4):
                    gre, gim, sign = gram_of(s0 + a, t)
                    if sign > 0:
                        accs[a] = accs[a] + gre * vx + gim * vy
                    else:
                        accs[a] = accs[a] + gre * vx - gim * vy
            for a in range(4):
                value = accs[a] if scale is None else accs[a] * scale * scale
                out_x[s0 + a] = value
                out_y[s0 + a] = turned(value)

    times_gram(sketch_of, lambda t: sky[t], px, py, scaling)
    times_gram(lambda t: px[t], lambda t: py[t], hx, hy, None)

    for j0 in range(0, SKETCH, 4):
        k0 = 8 * (j0 // 8)
        accs = [jnp.zeros((2, SKETCH - k0, LINES), jnp.float32) for _ in range(4)]
        for s in range(SEGMENTS):
            vx, vy = hx[s, :, k0:, :], hy[s, :, k0:, :]
            for a in range(4):
                accs[a] = accs[a] + px[s, 0, j0 + a:j0 + a + 1, :] * vx - px[s, 1, j0 + a:j0 + a + 1, :] * vy
        for a in range(4):
            gram[j0 + a, :, k0:, :] = accs[a]

    for j0 in range(0, SKETCH, 4):
        accs = [jnp.zeros((2, channels, LINES), jnp.float32) for _ in range(4)]
        for s in range(SEGMENTS):
            vx = jnp.stack([sre[s * channels:(s + 1) * channels, :], sim[s * channels:(s + 1) * channels, :]])
            vy = turned(vx)
            for a in range(4):
                accs[a] = accs[a] + px[s, 0, j0 + a:j0 + a + 1, :] * vx + px[s, 1, j0 + a:j0 + a + 1, :] * vy
        for a in range(4):
            basis[j0 + a] = accs[a]

    for i in range(SKETCH):
        k0 = 8 * (i // 8)
        columns = k0 + lax.broadcasted_iota(jnp.int32, (SKETCH - k0, LINES), 0)
        row = gram[i, :, k0:, :]
        diagonal = jnp.sqrt(gram[i, 0, i:i + 1, :])
        inverse = 1.0 / diagonal
        scaled = row * inverse
        re = jnp.where(columns > i, scaled[0], 0.0)
        re = jnp.where(columns == i, diagonal, re)
        im = jnp.where(columns > i, scaled[1], 0.0)
        value = jnp.stack([re, im])
        if k0:
            factor[0, i, :k0, :] = jnp.zeros((k0, LINES), jnp.float32)
            factor[1, i, :k0, :] = jnp.zeros((k0, LINES), jnp.float32)
        factor[0, i, k0:, :] = re
        factor[1, i, k0:, :] = im
        rows_x[i, :, k0:, :] = value
        mode = basis[i] * inverse
        modes[pl.ds(i, channels, stride=2 * SKETCH), :] = mode[0] * root
        modes[pl.ds(i + SKETCH, channels, stride=2 * SKETCH), :] = mode[1] * root
        other = turned(mode)
        for r in range(i + 1, SKETCH):
            r0 = 8 * (r // 8)
            top_re = rows_x[i, 0, r:r + 1, :]
            top_im = rows_x[i, 1, r:r + 1, :]
            late = value[:, r0 - k0:, :]
            gram[r, :, r0:, :] = gram[r, :, r0:, :] - (top_re * late - top_im * turned(late))
            basis[r] = basis[r] - (top_re * mode + top_im * other)


def finish(full, sre, sim, channels_all):
    channels = sre.shape[0] // SEGMENTS
    vmem = pl.BlockSpec(memory_space=pltpu.VMEM)
    kernel = functools.partial(mode_kernel, 1.0 / (SEGMENTS * channels_all), math.sqrt(channels_all))
    tall = pltpu.VMEM((SEGMENTS, 2, SKETCH, LINES), jnp.float32)
    wide = pltpu.VMEM((SKETCH, 2, SKETCH, LINES), jnp.float32)
    return pl.pallas_call(
        kernel,
        out_shape=[
            jax.ShapeDtypeStruct((channels * 2 * SKETCH, LINES), jnp.float32),
            jax.ShapeDtypeStruct((2, SKETCH, SKETCH, LINES), jnp.float32),
        ],
        in_specs=[vmem] * 3,
        out_specs=[vmem] * 2,
        scratch_shapes=[tall] * 5 + [wide] * 2 + [pltpu.VMEM((SKETCH, 2, channels, LINES), jnp.float32)],
        compiler_params=pltpu.CompilerParams(vmem_limit_bytes=48 * 1024 * 1024),
        name="modes",
    )(full, sre, sim)


def shards(dims, strain, band_start, sketch_seed):
    channels, samples = strain.shape
    channels_all = channels * lax.axis_size("ch")
    table = dft_table(band_start, samples // SEGMENTS, LINES)
    full, sre, sim = all_sums(dims, strain, table, sketch_seed)
    modes, factor = finish(full.reshape(2, HALF_ROWS, LINES), sre, sim, channels_all)
    return modes.reshape(channels, 2, SKETCH, LINES), factor


def solution(mesh, dims=(4, 4, 16)):
    in_specs = (P("ch", None), P(), P())
    out_specs = (P("ch", None, None, None), P())
    return jax.shard_map(
        functools.partial(shards, dims), mesh=mesh, in_specs=in_specs, out_specs=out_specs, check_vma=False
    )
```

```python
import functools
import math

import jax
import jax.numpy as jnp
from jax import lax
from jax.experimental import pallas as pl
from jax.experimental.pallas import tpu as pltpu
from jax.sharding import PartitionSpec as P

SEGMENTS = 24
LINES = 128
SKETCH = 16
HALF_ROWS = SEGMENTS * 2 * SKETCH
MESH = pl.DeviceIdType.MESH
GROUP = 4


def dft_table(band_start, segment_length, line_count):
    times_idx = jnp.arange(segment_length, dtype=jnp.int32)[:, None]
    line_ids = band_start[0] + jnp.arange(line_count, dtype=jnp.int32)[None, :]
    residues = times_idx * line_ids % segment_length
    phases = 2.0 * math.pi / segment_length * residues.astype(jnp.float32)
    window = 0.5 - 0.5 * jnp.cos(2.0 * math.pi / segment_length * times_idx.astype(jnp.float32))
    weighting = window / math.sqrt(3.0 * segment_length / 8.0)
    return jnp.concatenate(
        [weighting * jnp.cos(phases), -weighting * jnp.sin(phases)], axis=1
    ).astype(jnp.bfloat16)


def sign_block(first_channel, seed, channels, copies, group):
    shape = (group * 2 * SKETCH, group * copies * channels)
    row = lax.broadcasted_iota(jnp.int32, shape, 0)
    col = lax.broadcasted_iota(jnp.int32, shape, 1)
    inside = jnp.zeros(shape, jnp.bool_)
    for g in range(group):
        inside = inside | (
            (row >= g * 2 * SKETCH) & (row < (g + 1) * 2 * SKETCH)
            & (col >= g * copies * channels) & (col < (g + 1) * copies * channels)
        )
    channel = first_channel + jnp.bitwise_and(col, channels - 1)
    half = jnp.bitwise_and(lax.shift_right_logical(row, jnp.full_like(row, 4)), 1)
    column = jnp.bitwise_and(row, SKETCH - 1)
    hashed = (channel * SKETCH + column) * 2 + half + seed * 1000003
    hashed = hashed * -1640531535
    hashed = jnp.bitwise_xor(hashed, lax.shift_right_logical(hashed, jnp.full_like(hashed, 15)))
    hashed = hashed * 2146121005
    hashed = jnp.bitwise_xor(hashed, lax.shift_right_logical(hashed, jnp.full_like(hashed, 13)))
    bits = jnp.bitwise_and(lax.shift_right_logical(hashed, jnp.full_like(hashed, 7)), 1)
    return jnp.where(inside, (1 - 2 * bits).astype(jnp.float32), 0.0)


def gram_row(t, s, part):
    block = t // 8
    return 8 * (0, 16, 48)[block] + (t % 8) * 16 * (block + 1) + part * 8 * (block + 1) + s


def sum_kernel(dims, strain, table, seed, full_out, sre, sim,
               part, crecv, xrecv, zall, full,
               c_send, c_recv, x_send, x_recv, z_send, z_recv, a_send, a_recv, f_send, f_recv):
    nx, ny, nz = dims
    units = nx * ny * 2
    rows = HALF_ROWS // units
    channels = strain.shape[0]
    length = table.shape[0]

    me = lax.axis_index("ch")
    core = lax.rem(me, 2)
    z = lax.rem(lax.div(me, 2), nz)
    p = lax.div(me, 2 * nz)
    x, y = lax.div(p, ny), lax.rem(p, ny)
    odd, level = lax.rem(z, 2), lax.div(z, 2)
    mate = me + 1 - 2 * core
    here = p * 2 + odd

    def unit_at(d, sign):
        dx, dy, flip = d // 2 // ny, d // 2 % ny, d % 2
        qx = lax.rem(x + (dx if sign > 0 else nx - dx), nx)
        qy = lax.rem(y + (dy if sign > 0 else ny - dy), ny)
        return (qx * ny + qy) * 2 + (1 - odd if flip else odd)

    def hops(d):
        dx, dy = d // 2 // ny, d // 2 % ny
        return min(dx, nx - dx) + min(dy, ny - dy) + d % 2

    far_first = sorted(range(1, units), key=lambda d: (-hops(d), d))

    def unit_device(u):
        return lax.div(u, 2) * (2 * nz) + (level * 2 + lax.rem(u, 2)) * 2 + core

    def level_device(e):
        return p * (2 * nz) + (lax.rem(level + e, nz // 2) * 2 + odd) * 2 + core

    barrier = pltpu.get_barrier_semaphore()
    for e in range(1, nz // 2):
        pl.semaphore_signal(barrier, inc=1, device_id=(level_device(e),), device_id_type=MESH)
    for d in far_first:
        pl.semaphore_signal(barrier, inc=1, device_id=(unit_device(unit_at(d, 1)),), device_id_type=MESH)
    pl.semaphore_signal(barrier, inc=1, device_id=(mate,), device_id_type=MESH)

    def put(half, row, value):
        for r in range(row, row + value.shape[0], 8):
            part[half, r // rows, r % rows:r % rows + 8, :] = value[r - row:r - row + 8, :]

    def remote(src, dst, send, recv, device):
        return pltpu.make_async_remote_copy(
            src_ref=src, dst_ref=dst, send_sem=send, recv_sem=recv, device_id=(device,), device_id_type=MESH
        )

    flat = jnp.concatenate([strain[:, s * length:(s + 1) * length] for s in range(SEGMENTS)], axis=0)
    both = jnp.dot(flat, table[...], preferred_element_type=jnp.float32)
    sre[...] = both[:, :LINES]
    sim[...] = both[:, LINES:]

    signs = sign_block(me * channels, seed[0], channels, 3, GROUP).astype(jnp.bfloat16)
    for s0 in range(0, SEGMENTS, GROUP):
        terms = []
        for s in range(s0, s0 + GROUP):
            both = jnp.concatenate(
                [sre[s * channels:(s + 1) * channels, :], sim[s * channels:(s + 1) * channels, :]], axis=1
            )
            high = both.astype(jnp.bfloat16)
            rest = both - high.astype(jnp.float32)
            middle = rest.astype(jnp.bfloat16)
            low = (rest - middle.astype(jnp.float32)).astype(jnp.bfloat16)
            terms += [high, middle, low]
        prods = jnp.dot(signs, jnp.concatenate(terms, axis=0), preferred_element_type=jnp.float32)
        for s in range(s0, s0 + GROUP):
            prod = prods[(s - s0) * 2 * SKETCH:(s - s0 + 1) * 2 * SKETCH, :]
            for half, value in enumerate((
                prod[:SKETCH, :LINES] + prod[SKETCH:, LINES:],
                prod[SKETCH:, :LINES] - prod[:SKETCH, LINES:],
            )):
                row = s * 2 * SKETCH + half * SKETCH
                put(0, row, value)

    pl.semaphore_wait(barrier, units + nz // 2 - 1)

    def landed(ref, sem):
        pltpu.make_async_copy(ref, ref, sem).wait()

    def pair(half, q, count):
        span = pl.ds(q, count)
        return remote(part.at[half, span], crecv.at[span], c_send, c_recv, mate)

    @pl.when(core == 1)
    def _():
        pair(0, 0, units).start()

    sent = units
    for t0 in range(SEGMENTS - 4, -1, -4):
        n = 8 * (t0 // 8 + 1)
        zero = jnp.zeros((n, LINES), jnp.float32)
        accs = [zero] * 8
        for c in range(channels):
            vre = sre[pl.ds(c, n, stride=channels), :]
            vim = sim[pl.ds(c, n, stride=channels), :]
            for a in range(4):
                bre = sre[(t0 + a) * channels + c:(t0 + a) * channels + c + 1, :]
                bim = sim[(t0 + a) * channels + c:(t0 + a) * channels + c + 1, :]
                accs[2 * a] += vre * bre + vim * bim
                accs[2 * a + 1] += vre * bim - vim * bre
        for a in range(4):
            for half in range(2):
                for tile in range(n // 8):
                    row = gram_row(t0 + a, 8 * tile, half)
                    put(1, row, accs[2 * a + half][8 * tile:8 * tile + 8, :])
        first = -(-gram_row(t0, 0, 0) // rows)

        if first < sent:
            @pl.when(core == 0)
            def _(first=first, count=sent - first):
                pair(1, first, count).start()
        sent = min(sent, first)

    landed(crecv, c_recv)
    for d in far_first:
        u = unit_at(d, 1)
        crecv[u] = crecv[u] + part[core, u]
        remote(crecv.at[u], xrecv.at[d], x_send, x_recv, unit_device(u)).start()
    total = crecv[here] + part[core, here]
    landed(xrecv.at[pl.ds(1, units - 1)], x_recv)
    for d in range(1, units):
        total = total + xrecv[d]
    zall[level] = total
    for e in range(1, nz // 2):
        remote(zall.at[level], zall.at[level], z_send, z_recv, level_device(e)).start()
    landed(zall.at[pl.ds(1, nz // 2 - 1)], z_recv)
    total = zall[0]
    for e in range(1, nz // 2):
        total = total + zall[e]
    full[core, here] = total
    for d in far_first:
        remote(full.at[core, here], full.at[core, here], a_send, a_recv.at[d], unit_device(unit_at(d, 1))).start()
    for d in [0] + far_first:
        u = unit_at(d, -1)
        if d:
            remote(full.at[core, u], full.at[core, u], a_send, a_recv.at[d], unit_device(u)).wait_recv()
        remote(full.at[core, u], full.at[core, u], f_send, f_recv, mate).start()
    landed(full.at[1 - core], f_recv)
    landed(full.at[core], f_send)
    landed(crecv, c_send)
    landed(zall.at[pl.ds(1, nz // 2 - 1)], z_send)
    landed(xrecv.at[pl.ds(1, units - 1)], x_send)
    landed(xrecv.at[pl.ds(1, units - 1)], a_send)
    full_out[...] = full[...]


def all_sums(dims, strain, table, seed):
    nx, ny, nz = dims
    units = nx * ny * 2
    rows = HALF_ROWS // units
    channels = strain.shape[0]
    vmem = pl.BlockSpec(memory_space=pltpu.VMEM)
    dma = pltpu.SemaphoreType.DMA
    spectrum = jax.ShapeDtypeStruct((SEGMENTS * channels, LINES), jnp.float32)
    return pl.pallas_call(
        functools.partial(sum_kernel, dims),
        out_shape=[jax.ShapeDtypeStruct((2, units, rows, LINES), jnp.float32), spectrum, spectrum],
        in_specs=[vmem, vmem, pl.BlockSpec(memory_space=pltpu.SMEM)],
        out_specs=[vmem, vmem, vmem],
        scratch_shapes=[
            pltpu.VMEM((2, units, rows, LINES), jnp.float32),
            pltpu.VMEM((units, rows, LINES), jnp.float32),
            pltpu.VMEM((units, rows, LINES), jnp.float32),
            pltpu.VMEM((nz // 2, rows, LINES), jnp.float32),
            pltpu.VMEM((2, units, rows, LINES), jnp.float32),
        ] + [dma(())] * 7 + [dma((units,)), dma(()), dma(())],
        compiler_params=pltpu.CompilerParams(
            collective_id=0, has_side_effects=True, vmem_limit_bytes=48 * 1024 * 1024
        ),
        name="sums",
    )(strain, table, seed)


def mode_kernel(scaling, root, full, sre, sim, modes, factor, sky, px, py, hx, hy, gram, rows_x, basis):
    channels = sre.shape[0] // SEGMENTS

    def turned(value):
        return jnp.stack([-value[1], value[0]])

    def sketch_of(t):
        row = t * 2 * SKETCH
        return jnp.stack([full[0, row:row + SKETCH, :], full[0, row + SKETCH:row + 2 * SKETCH, :]])

    def gram_of(s, t):
        if s // 8 <= t // 8:
            first, second, sign = t, s, 1
        else:
            first, second, sign = s, t, -1
        row = gram_row(first, second, 0)
        row_im = gram_row(first, second, 1)
        return full[1, row:row + 1, :], full[1, row_im:row_im + 1, :], sign

    for t in range(SEGMENTS):
        sky[t] = turned(sketch_of(t))

    def times_gram(get_x, get_y, out_x, out_y, scale):
        for s0 in range(0, SEGMENTS, 4):
            accs = [jnp.zeros((2, SKETCH, LINES), jnp.float32) for _ in range(4)]
            for t in range(SEGMENTS):
                vx, vy = get_x(t), get_y(t)
                for a in range(4):
                    gre, gim, sign = gram_of(s0 + a, t)
                    if sign > 0:
                        accs[a] = accs[a] + gre * vx + gim * vy
                    else:
                        accs[a] = accs[a] + gre * vx - gim * vy
            for a in range(4):
                value = accs[a] if scale is None else accs[a] * scale * scale
                out_x[s0 + a] = value
                out_y[s0 + a] = turned(value)

    times_gram(sketch_of, lambda t: sky[t], px, py, scaling)
    times_gram(lambda t: px[t], lambda t: py[t], hx, hy, None)

    for j0 in range(0, SKETCH, 4):
        k0 = 8 * (j0 // 8)
        accs = [jnp.zeros((2, SKETCH - k0, LINES), jnp.float32) for _ in range(4)]
        for s in range(SEGMENTS):
            vx, vy = hx[s, :, k0:, :], hy[s, :, k0:, :]
            for a in range(4):
                accs[a] = accs[a] + px[s, 0, j0 + a:j0 + a + 1, :] * vx - px[s, 1, j0 + a:j0 + a + 1, :] * vy
        for a in range(4):
            gram[j0 + a, :, k0:, :] = accs[a]

    for j0 in range(0, SKETCH, 4):
        accs = [jnp.zeros((2, channels, LINES), jnp.float32) for _ in range(4)]
        for s in range(SEGMENTS):
            vx = jnp.stack([sre[s * channels:(s + 1) * channels, :], sim[s * channels:(s + 1) * channels, :]])
            vy = turned(vx)
            for a in range(4):
                accs[a] = accs[a] + px[s, 0, j0 + a:j0 + a + 1, :] * vx + px[s, 1, j0 + a:j0 + a + 1, :] * vy
        for a in range(4):
            basis[j0 + a] = accs[a]

    for i in range(SKETCH):
        k0 = 8 * (i // 8)
        columns = k0 + lax.broadcasted_iota(jnp.int32, (SKETCH - k0, LINES), 0)
        row = gram[i, :, k0:, :]
        diagonal = jnp.sqrt(gram[i, 0, i:i + 1, :])
        inverse = 1.0 / diagonal
        scaled = row * inverse
        re = jnp.where(columns > i, scaled[0], 0.0)
        re = jnp.where(columns == i, diagonal, re)
        im = jnp.where(columns > i, scaled[1], 0.0)
        value = jnp.stack([re, im])
        if k0:
            factor[0, i, :k0, :] = jnp.zeros((k0, LINES), jnp.float32)
            factor[1, i, :k0, :] = jnp.zeros((k0, LINES), jnp.float32)
        factor[0, i, k0:, :] = re
        factor[1, i, k0:, :] = im
        rows_x[i, :, k0:, :] = value
        mode = basis[i] * inverse
        modes[pl.ds(i, channels, stride=2 * SKETCH), :] = mode[0] * root
        modes[pl.ds(i + SKETCH, channels, stride=2 * SKETCH), :] = mode[1] * root
        other = turned(mode)
        for r in range(i + 1, SKETCH):
            r0 = 8 * (r // 8)
            top_re = rows_x[i, 0, r:r + 1, :]
            top_im = rows_x[i, 1, r:r + 1, :]
            late = value[:, r0 - k0:, :]
            gram[r, :, r0:, :] = gram[r, :, r0:, :] - (top_re * late - top_im * turned(late))
            basis[r] = basis[r] - (top_re * mode + top_im * other)


def finish(full, sre, sim, channels_all):
    channels = sre.shape[0] // SEGMENTS
    vmem = pl.BlockSpec(memory_space=pltpu.VMEM)
    kernel = functools.partial(mode_kernel, 1.0 / (SEGMENTS * channels_all), math.sqrt(channels_all))
    tall = pltpu.VMEM((SEGMENTS, 2, SKETCH, LINES), jnp.float32)
    wide = pltpu.VMEM((SKETCH, 2, SKETCH, LINES), jnp.float32)
    return pl.pallas_call(
        kernel,
        out_shape=[
            jax.ShapeDtypeStruct((channels * 2 * SKETCH, LINES), jnp.float32),
            jax.ShapeDtypeStruct((2, SKETCH, SKETCH, LINES), jnp.float32),
        ],
        in_specs=[vmem] * 3,
        out_specs=[vmem] * 2,
        scratch_shapes=[tall] * 5 + [wide] * 2 + [pltpu.VMEM((SKETCH, 2, channels, LINES), jnp.float32)],
        compiler_params=pltpu.CompilerParams(vmem_limit_bytes=48 * 1024 * 1024),
        name="modes",
    )(full, sre, sim)


def shards(dims, strain, band_start, sketch_seed):
    channels, samples = strain.shape
    channels_all = channels * lax.axis_size("ch")
    table = dft_table(band_start, samples // SEGMENTS, LINES)
    full, sre, sim = all_sums(dims, strain, table, sketch_seed)
    modes, factor = finish(full.reshape(2, HALF_ROWS, LINES), sre, sim, channels_all)
    return modes.reshape(channels, 2, SKETCH, LINES), factor


def solution(mesh, dims=(4, 4, 16)):
    in_specs = (P("ch", None), P(), P())
    out_specs = (P("ch", None, None, None), P())
    return jax.shard_map(
        functools.partial(shards, dims), mesh=mesh, in_specs=in_specs, out_specs=out_specs, check_vma=False
    )
```

```python
import functools
import math

import jax
import jax.numpy as jnp
from jax import lax
from jax.experimental import pallas as pl
from jax.experimental.pallas import tpu as pltpu
from jax.sharding import PartitionSpec as P

SEGMENTS = 24
LINES = 128
SKETCH = 16
HALF_ROWS = SEGMENTS * 2 * SKETCH
MESH = pl.DeviceIdType.MESH
GROUP = 4


def dft_table(band_start, segment_length, line_count):
    times_idx = jnp.arange(segment_length, dtype=jnp.int32)[:, None]
    line_ids = band_start[0] + jnp.arange(line_count, dtype=jnp.int32)[None, :]
    residues = times_idx * line_ids % segment_length
    phases = 2.0 * math.pi / segment_length * residues.astype(jnp.float32)
    window = 0.5 - 0.5 * jnp.cos(2.0 * math.pi / segment_length * times_idx.astype(jnp.float32))
    weighting = window / math.sqrt(3.0 * segment_length / 8.0)
    return jnp.concatenate(
        [weighting * jnp.cos(phases), -weighting * jnp.sin(phases)], axis=1
    ).astype(jnp.bfloat16)


def sign_block(first_channel, seed, channels, copies, group):
    shape = (group * 2 * SKETCH, group * copies * channels)
    row = lax.broadcasted_iota(jnp.int32, shape, 0)
    col = lax.broadcasted_iota(jnp.int32, shape, 1)
    inside = jnp.zeros(shape, jnp.bool_)
    for g in range(group):
        inside = inside | (
            (row >= g * 2 * SKETCH) & (row < (g + 1) * 2 * SKETCH)
            & (col >= g * copies * channels) & (col < (g + 1) * copies * channels)
        )
    channel = first_channel + jnp.bitwise_and(col, channels - 1)
    half = jnp.bitwise_and(lax.shift_right_logical(row, jnp.full_like(row, 4)), 1)
    column = jnp.bitwise_and(row, SKETCH - 1)
    hashed = (channel * SKETCH + column) * 2 + half + seed * 1000003
    hashed = hashed * -1640531535
    hashed = jnp.bitwise_xor(hashed, lax.shift_right_logical(hashed, jnp.full_like(hashed, 15)))
    hashed = hashed * 2146121005
    hashed = jnp.bitwise_xor(hashed, lax.shift_right_logical(hashed, jnp.full_like(hashed, 13)))
    bits = jnp.bitwise_and(lax.shift_right_logical(hashed, jnp.full_like(hashed, 7)), 1)
    return jnp.where(inside, (1 - 2 * bits).astype(jnp.float32), 0.0)


def gram_row(t, s, part):
    block = t // 8
    return 8 * (0, 16, 48)[block] + (t % 8) * 16 * (block + 1) + part * 8 * (block + 1) + s


def sum_kernel(dims, strain, table, seed, full_out, sre, sim,
               part, crecv, xrecv, zall, full,
               c_send, c_recv, x_send, x_recv, z_send, z_recv, a_send, a_recv, f_send, f_recv):
    nx, ny, nz = dims
    units = nx * ny * 2
    rows = HALF_ROWS // units
    channels = strain.shape[0]
    length = table.shape[0]

    me = lax.axis_index("ch")
    core = lax.rem(me, 2)
    z = lax.rem(lax.div(me, 2), nz)
    p = lax.div(me, 2 * nz)
    x, y = lax.div(p, ny), lax.rem(p, ny)
    odd, level = lax.rem(z, 2), lax.div(z, 2)
    mate = me + 1 - 2 * core
    here = p * 2 + odd

    def unit_at(d, sign):
        dx, dy, flip = d // 2 // ny, d // 2 % ny, d % 2
        qx = lax.rem(x + (dx if sign > 0 else nx - dx), nx)
        qy = lax.rem(y + (dy if sign > 0 else ny - dy), ny)
        return (qx * ny + qy) * 2 + (1 - odd if flip else odd)

    def hops(d):
        dx, dy = d // 2 // ny, d // 2 % ny
        return min(dx, nx - dx) + min(dy, ny - dy) + d % 2

    far_first = sorted(range(1, units), key=lambda d: (-hops(d), d))

    def unit_device(u):
        return lax.div(u, 2) * (2 * nz) + (level * 2 + lax.rem(u, 2)) * 2 + core

    def level_device(e):
        return p * (2 * nz) + (lax.rem(level + e, nz // 2) * 2 + odd) * 2 + core

    barrier = pltpu.get_barrier_semaphore()
    for e in range(1, nz // 2):
        pl.semaphore_signal(barrier, inc=1, device_id=(level_device(e),), device_id_type=MESH)
    for d in far_first:
        pl.semaphore_signal(barrier, inc=1, device_id=(unit_device(unit_at(d, 1)),), device_id_type=MESH)
    pl.semaphore_signal(barrier, inc=1, device_id=(mate,), device_id_type=MESH)

    def put(half, row, value):
        for r in range(row, row + value.shape[0], 8):
            part[half, r // rows, r % rows:r % rows + 8, :] = value[r - row:r - row + 8, :]

    def remote(src, dst, send, recv, device):
        return pltpu.make_async_remote_copy(
            src_ref=src, dst_ref=dst, send_sem=send, recv_sem=recv, device_id=(device,), device_id_type=MESH
        )

    flat = jnp.concatenate([strain[:, s * length:(s + 1) * length] for s in range(SEGMENTS)], axis=0)
    both = jnp.dot(flat, table[...], preferred_element_type=jnp.float32)
    sre[...] = both[:, :LINES]
    sim[...] = both[:, LINES:]

    signs = sign_block(me * channels, seed[0], channels, 3, GROUP).astype(jnp.bfloat16)
    for s0 in range(0, SEGMENTS, GROUP):
        terms = []
        for s in range(s0, s0 + GROUP):
            both = jnp.concatenate(
                [sre[s * channels:(s + 1) * channels, :], sim[s * channels:(s + 1) * channels, :]], axis=1
            )
            high = both.astype(jnp.bfloat16)
            rest = both - high.astype(jnp.float32)
            middle = rest.astype(jnp.bfloat16)
            low = (rest - middle.astype(jnp.float32)).astype(jnp.bfloat16)
            terms += [high, middle, low]
        prods = jnp.dot(signs, jnp.concatenate(terms, axis=0), preferred_element_type=jnp.float32)
        for s in range(s0, s0 + GROUP):
            prod = prods[(s - s0) * 2 * SKETCH:(s - s0 + 1) * 2 * SKETCH, :]
            for half, value in enumerate((
                prod[:SKETCH, :LINES] + prod[SKETCH:, LINES:],
                prod[SKETCH:, :LINES] - prod[:SKETCH, LINES:],
            )):
                row = s * 2 * SKETCH + half * SKETCH
                put(0, row, value)

    pl.semaphore_wait(barrier, units + nz // 2 - 1)

    def landed(ref, sem):
        pltpu.make_async_copy(ref, ref, sem).wait()

    def pair(half, q, count):
        span = pl.ds(q, count)
        return remote(part.at[half, span], crecv.at[span], c_send, c_recv, mate)

    @pl.when(core == 1)
    def _():
        pair(0, 0, units).start()

    sent = units
    for t0 in range(SEGMENTS - 4, -1, -4):
        n = 8 * (t0 // 8 + 1)
        zero = jnp.zeros((n, LINES), jnp.float32)
        accs = [zero] * 8
        for c in range(channels):
            vre = sre[pl.ds(c, n, stride=channels), :]
            vim = sim[pl.ds(c, n, stride=channels), :]
            for a in range(4):
                bre = sre[(t0 + a) * channels + c:(t0 + a) * channels + c + 1, :]
                bim = sim[(t0 + a) * channels + c:(t0 + a) * channels + c + 1, :]
                accs[2 * a] += vre * bre + vim * bim
                accs[2 * a + 1] += vre * bim - vim * bre
        for a in range(4):
            for half in range(2):
                for tile in range(n // 8):
                    row = gram_row(t0 + a, 8 * tile, half)
                    put(1, row, accs[2 * a + half][8 * tile:8 * tile + 8, :])
        first = -(-gram_row(t0, 0, 0) // rows)

        if first < sent:
            @pl.when(core == 0)
            def _(first=first, count=sent - first):
                pair(1, first, count).start()
        sent = min(sent, first)

    landed(crecv, c_recv)
    for d in far_first:
        u = unit_at(d, 1)
        crecv[u] = crecv[u] + part[core, u]
        remote(crecv.at[u], xrecv.at[d], x_send, x_recv, unit_device(u)).start()
    total = crecv[here] + part[core, here]
    landed(xrecv.at[pl.ds(1, units - 1)], x_recv)
    for d in range(1, units):
        total = total + xrecv[d]
    zall[level] = total
    for e in range(1, nz // 2):
        remote(zall.at[level], zall.at[level], z_send, z_recv, level_device(e)).start()
    landed(zall.at[pl.ds(1, nz // 2 - 1)], z_recv)
    total = zall[0]
    for e in range(1, nz // 2):
        total = total + zall[e]
    full[core, here] = total
    for d in far_first:
        remote(full.at[core, here], full.at[core, here], a_send, a_recv.at[d], unit_device(unit_at(d, 1))).start()
    for d in [0] + far_first:
        u = unit_at(d, -1)
        if d:
            remote(full.at[core, u], full.at[core, u], a_send, a_recv.at[d], unit_device(u)).wait_recv()
        remote(full.at[core, u], full.at[core, u], f_send, f_recv, mate).start()
    landed(full.at[1 - core], f_recv)
    landed(full.at[core], f_send)
    landed(crecv, c_send)
    landed(zall.at[pl.ds(1, nz // 2 - 1)], z_send)
    landed(xrecv.at[pl.ds(1, units - 1)], x_send)
    landed(xrecv.at[pl.ds(1, units - 1)], a_send)
    full_out[...] = full[...]


def all_sums(dims, strain, table, seed):
    nx, ny, nz = dims
    units = nx * ny * 2
    rows = HALF_ROWS // units
    channels = strain.shape[0]
    vmem = pl.BlockSpec(memory_space=pltpu.VMEM)
    dma = pltpu.SemaphoreType.DMA
    spectrum = jax.ShapeDtypeStruct((SEGMENTS * channels, LINES), jnp.float32)
    return pl.pallas_call(
        functools.partial(sum_kernel, dims),
        out_shape=[jax.ShapeDtypeStruct((2, units, rows, LINES), jnp.float32), spectrum, spectrum],
        in_specs=[vmem, vmem, pl.BlockSpec(memory_space=pltpu.SMEM)],
        out_specs=[vmem, vmem, vmem],
        scratch_shapes=[
            pltpu.VMEM((2, units, rows, LINES), jnp.float32),
            pltpu.VMEM((units, rows, LINES), jnp.float32),
            pltpu.VMEM((units, rows, LINES), jnp.float32),
            pltpu.VMEM((nz // 2, rows, LINES), jnp.float32),
            pltpu.VMEM((2, units, rows, LINES), jnp.float32),
        ] + [dma(())] * 7 + [dma((units,)), dma(()), dma(())],
        compiler_params=pltpu.CompilerParams(
            collective_id=0, has_side_effects=True, vmem_limit_bytes=48 * 1024 * 1024
        ),
        name="sums",
    )(strain, table, seed)


def mode_kernel(scaling, root, full, sre, sim, modes, factor, gsum, sksum, px, psum, pdiff, hx, hsum, ssum, gram, rows_x, basis):
    channels = sre.shape[0] // SEGMENTS

    def turned(value):
        return jnp.stack([-value[1], value[0]])

    for t in range(SEGMENTS):
        n = 8 * (t // 8 + 1)
        re = full[1, gram_row(t, 0, 0):gram_row(t, 0, 0) + n, :]
        im = full[1, gram_row(t, 0, 1):gram_row(t, 0, 1) + n, :]
        gsum[0, t, :n, :] = re + im
        gsum[1, t, :n, :] = re - im
    for t in range(SEGMENTS):
        row = t * 2 * SKETCH
        sksum[t] = full[0, row:row + SKETCH, :] + full[0, row + SKETCH:row + 2 * SKETCH, :]

    def sketch_of(t):
        row = t * 2 * SKETCH
        return full[0, row:row + SKETCH, :], full[0, row + SKETCH:row + 2 * SKETCH, :], sksum[t]

    def gram_of(s, t):
        sign = s // 8 <= t // 8
        first, second = (t, s) if sign else (s, t)
        row = gram_row(first, second, 0)
        row_im = gram_row(first, second, 1)
        third = gsum[0 if sign else 1, first, second:second + 1, :]
        return full[1, row:row + 1, :], full[1, row_im:row_im + 1, :], third, sign

    def sums(count, shape, left, right):
        accs = [[jnp.zeros(shape, jnp.float32) for _ in range(4)] for _ in range(count)]
        kinds = [set() for _ in range(count)]
        for s in range(SEGMENTS):
            vre, vim, vsum = right(s)
            for a in range(count):
                lre, lim, third, straight = left(s, a)
                kinds[a].add(straight)
                accs[a][0] = accs[a][0] + lre * vre
                if straight:
                    accs[a][1] = accs[a][1] + lim * vim
                else:
                    accs[a][2] = accs[a][2] + lim * vim
                accs[a][3] = accs[a][3] + third * vsum
        out = []
        for a in range(count):
            prod_re, straight, conjugate, both = accs[a]
            im = both - prod_re
            re = prod_re
            if True in kinds[a]:
                im, re = im - straight, re - straight
            if False in kinds[a]:
                im, re = im + conjugate, re + conjugate
            out.append((re, im))
        return out

    def times_gram(right, scale, store):
        for s0 in range(0, SEGMENTS, 4):
            for a, (re, im) in enumerate(sums(4, (SKETCH, LINES), lambda t, a: gram_of(s0 + a, t), right)):
                store(s0 + a, re if scale is None else re * scale * scale, im if scale is None else im * scale * scale)

    def store_p(s, re, im):
        px[s, 0] = re
        px[s, 1] = im
        psum[s] = re + im
        pdiff[s] = re - im

    def store_h(s, re, im):
        hx[s, 0] = re
        hx[s, 1] = im
        hsum[s] = re + im

    times_gram(sketch_of, scaling, store_p)
    times_gram(lambda t: (px[t, 0], px[t, 1], psum[t]), None, store_h)

    for j0 in range(0, SKETCH, 4):
        k0 = 8 * (j0 // 8)

        def left(s, a):
            j = j0 + a
            return px[s, 0, j:j + 1, :], px[s, 1, j:j + 1, :], pdiff[s, j:j + 1, :], False

        right = lambda s: (hx[s, 0, k0:, :], hx[s, 1, k0:, :], hsum[s, k0:, :])
        for a, (re, im) in enumerate(sums(4, (SKETCH - k0, LINES), left, right)):
            gram[j0 + a, 0, k0:, :] = re
            gram[j0 + a, 1, k0:, :] = im

    ssum[...] = sre[...] + sim[...]
    for j0 in range(0, SKETCH, 4):

        def left(s, a):
            j = j0 + a
            return px[s, 0, j:j + 1, :], px[s, 1, j:j + 1, :], psum[s, j:j + 1, :], True

        def right(s):
            span = slice(s * channels, (s + 1) * channels)
            return sre[span, :], sim[span, :], ssum[span, :]

        for a, (re, im) in enumerate(sums(4, (channels, LINES), left, right)):
            basis[j0 + a, 0] = re
            basis[j0 + a, 1] = im

    for i in range(SKETCH):
        k0 = 8 * (i // 8)
        columns = k0 + lax.broadcasted_iota(jnp.int32, (SKETCH - k0, LINES), 0)
        row = gram[i, :, k0:, :]
        diagonal = jnp.sqrt(gram[i, 0, i:i + 1, :])
        inverse = 1.0 / diagonal
        scaled = row * inverse
        re = jnp.where(columns > i, scaled[0], 0.0)
        re = jnp.where(columns == i, diagonal, re)
        im = jnp.where(columns > i, scaled[1], 0.0)
        value = jnp.stack([re, im])
        if k0:
            factor[0, i, :k0, :] = jnp.zeros((k0, LINES), jnp.float32)
            factor[1, i, :k0, :] = jnp.zeros((k0, LINES), jnp.float32)
        factor[0, i, k0:, :] = re
        factor[1, i, k0:, :] = im
        rows_x[i, :, k0:, :] = value
        mode = basis[i] * inverse
        modes[pl.ds(i, channels, stride=2 * SKETCH), :] = mode[0] * root
        modes[pl.ds(i + SKETCH, channels, stride=2 * SKETCH), :] = mode[1] * root
        other = turned(mode)
        for r in range(i + 1, SKETCH):
            r0 = 8 * (r // 8)
            top_re = rows_x[i, 0, r:r + 1, :]
            top_im = rows_x[i, 1, r:r + 1, :]
            late = value[:, r0 - k0:, :]
            gram[r, :, r0:, :] = gram[r, :, r0:, :] - (top_re * late - top_im * turned(late))
            basis[r] = basis[r] - (top_re * mode + top_im * other)


def finish(full, sre, sim, channels_all):
    channels = sre.shape[0] // SEGMENTS
    vmem = pl.BlockSpec(memory_space=pltpu.VMEM)
    kernel = functools.partial(mode_kernel, 1.0 / (SEGMENTS * channels_all), math.sqrt(channels_all))
    tall = pltpu.VMEM((SEGMENTS, 2, SKETCH, LINES), jnp.float32)
    short = pltpu.VMEM((SEGMENTS, SKETCH, LINES), jnp.float32)
    wide = pltpu.VMEM((SKETCH, 2, SKETCH, LINES), jnp.float32)
    return pl.pallas_call(
        kernel,
        out_shape=[
            jax.ShapeDtypeStruct((channels * 2 * SKETCH, LINES), jnp.float32),
            jax.ShapeDtypeStruct((2, SKETCH, SKETCH, LINES), jnp.float32),
        ],
        in_specs=[vmem] * 3,
        out_specs=[vmem] * 2,
        scratch_shapes=[
            pltpu.VMEM((2, SEGMENTS, SEGMENTS, LINES), jnp.float32), short, tall, short, short, tall, short,
            pltpu.VMEM((SEGMENTS * channels, LINES), jnp.float32),
            wide, wide, pltpu.VMEM((SKETCH, 2, channels, LINES), jnp.float32),
        ],
        compiler_params=pltpu.CompilerParams(vmem_limit_bytes=48 * 1024 * 1024),
        name="modes",
    )(full, sre, sim)


def shards(dims, strain, band_start, sketch_seed):
    channels, samples = strain.shape
    channels_all = channels * lax.axis_size("ch")
    table = dft_table(band_start, samples // SEGMENTS, LINES)
    full, sre, sim = all_sums(dims, strain, table, sketch_seed)
    modes, factor = finish(full.reshape(2, HALF_ROWS, LINES), sre, sim, channels_all)
    return modes.reshape(channels, 2, SKETCH, LINES), factor


def solution(mesh, dims=(4, 4, 16)):
    in_specs = (P("ch", None), P(), P())
    out_specs = (P("ch", None, None, None), P())
    return jax.shard_map(
        functools.partial(shards, dims), mesh=mesh, in_specs=in_specs, out_specs=out_specs, check_vma=False
    )
```

```python
import functools
import math

import jax
import jax.numpy as jnp
from jax import lax
from jax.experimental import pallas as pl
from jax.experimental.pallas import tpu as pltpu
from jax.sharding import PartitionSpec as P

SEGMENTS = 24
LINES = 128
SKETCH = 16
HALF_ROWS = SEGMENTS * 2 * SKETCH
MESH = pl.DeviceIdType.MESH
GROUP = 4


def dft_table(band_start, segment_length, line_count):
    times_idx = jnp.arange(segment_length, dtype=jnp.int32)[:, None]
    line_ids = band_start[0] + jnp.arange(line_count, dtype=jnp.int32)[None, :]
    residues = times_idx * line_ids % segment_length
    phases = 2.0 * math.pi / segment_length * residues.astype(jnp.float32)
    window = 0.5 - 0.5 * jnp.cos(2.0 * math.pi / segment_length * times_idx.astype(jnp.float32))
    weighting = window / math.sqrt(3.0 * segment_length / 8.0)
    return jnp.concatenate(
        [weighting * jnp.cos(phases), -weighting * jnp.sin(phases)], axis=1
    ).astype(jnp.bfloat16)


def sign_block(first_channel, seed, channels, copies, group):
    shape = (group * 2 * SKETCH, group * copies * channels)
    row = lax.broadcasted_iota(jnp.int32, shape, 0)
    col = lax.broadcasted_iota(jnp.int32, shape, 1)
    inside = jnp.zeros(shape, jnp.bool_)
    for g in range(group):
        inside = inside | (
            (row >= g * 2 * SKETCH) & (row < (g + 1) * 2 * SKETCH)
            & (col >= g * copies * channels) & (col < (g + 1) * copies * channels)
        )
    channel = first_channel + jnp.bitwise_and(col, channels - 1)
    half = jnp.bitwise_and(lax.shift_right_logical(row, jnp.full_like(row, 4)), 1)
    column = jnp.bitwise_and(row, SKETCH - 1)
    hashed = (channel * SKETCH + column) * 2 + half + seed * 1000003
    hashed = hashed * -1640531535
    hashed = jnp.bitwise_xor(hashed, lax.shift_right_logical(hashed, jnp.full_like(hashed, 15)))
    hashed = hashed * 2146121005
    hashed = jnp.bitwise_xor(hashed, lax.shift_right_logical(hashed, jnp.full_like(hashed, 13)))
    bits = jnp.bitwise_and(lax.shift_right_logical(hashed, jnp.full_like(hashed, 7)), 1)
    return jnp.where(inside, (1 - 2 * bits).astype(jnp.float32), 0.0)


def gram_row(t, s, part):
    block = t // 8
    return 8 * (0, 16, 48)[block] + (t % 8) * 16 * (block + 1) + part * 8 * (block + 1) + s


def sum_kernel(dims, strain, table, seed, full_out, sre, sim,
               part, crecv, xrecv, zall, full,
               c_send, c_recv, x_send, x_recv, z_send, z_recv, a_send, a_recv, f_send, f_recv):
    nx, ny, nz = dims
    units = nx * ny * 2
    rows = HALF_ROWS // units
    channels = strain.shape[0]
    length = table.shape[0]

    me = lax.axis_index("ch")
    core = lax.rem(me, 2)
    z = lax.rem(lax.div(me, 2), nz)
    p = lax.div(me, 2 * nz)
    x, y = lax.div(p, ny), lax.rem(p, ny)
    odd, level = lax.rem(z, 2), lax.div(z, 2)
    mate = me + 1 - 2 * core
    here = p * 2 + odd

    def unit_at(d, sign):
        dx, dy, flip = d // 2 // ny, d // 2 % ny, d % 2
        qx = lax.rem(x + (dx if sign > 0 else nx - dx), nx)
        qy = lax.rem(y + (dy if sign > 0 else ny - dy), ny)
        return (qx * ny + qy) * 2 + (1 - odd if flip else odd)

    def hops(d):
        dx, dy = d // 2 // ny, d // 2 % ny
        return min(dx, nx - dx) + min(dy, ny - dy) + d % 2

    far_first = sorted(range(1, units), key=lambda d: (-hops(d), d))

    def unit_device(u):
        return lax.div(u, 2) * (2 * nz) + (level * 2 + lax.rem(u, 2)) * 2 + core

    def level_device(e):
        return p * (2 * nz) + (lax.rem(level + e, nz // 2) * 2 + odd) * 2 + core

    barrier = pltpu.get_barrier_semaphore()
    for e in range(1, nz // 2):
        pl.semaphore_signal(barrier, inc=1, device_id=(level_device(e),), device_id_type=MESH)
    for d in far_first:
        pl.semaphore_signal(barrier, inc=1, device_id=(unit_device(unit_at(d, 1)),), device_id_type=MESH)
    pl.semaphore_signal(barrier, inc=1, device_id=(mate,), device_id_type=MESH)

    def put(half, row, value):
        for r in range(row, row + value.shape[0], 8):
            part[half, r // rows, r % rows:r % rows + 8, :] = value[r - row:r - row + 8, :]

    def remote(src, dst, send, recv, device):
        return pltpu.make_async_remote_copy(
            src_ref=src, dst_ref=dst, send_sem=send, recv_sem=recv, device_id=(device,), device_id_type=MESH
        )

    flat = jnp.concatenate([strain[:, s * length:(s + 1) * length] for s in range(SEGMENTS)], axis=0)
    both = jnp.dot(flat, table[...], preferred_element_type=jnp.float32)
    sre[...] = both[:, :LINES]
    sim[...] = both[:, LINES:]

    signs = sign_block(me * channels, seed[0], channels, 3, GROUP).astype(jnp.bfloat16)
    for s0 in range(0, SEGMENTS, GROUP):
        terms = []
        for s in range(s0, s0 + GROUP):
            both = jnp.concatenate(
                [sre[s * channels:(s + 1) * channels, :], sim[s * channels:(s + 1) * channels, :]], axis=1
            )
            high = both.astype(jnp.bfloat16)
            rest = both - high.astype(jnp.float32)
            middle = rest.astype(jnp.bfloat16)
            low = (rest - middle.astype(jnp.float32)).astype(jnp.bfloat16)
            terms += [high, middle, low]
        prods = jnp.dot(signs, jnp.concatenate(terms, axis=0), preferred_element_type=jnp.float32)
        for s in range(s0, s0 + GROUP):
            prod = prods[(s - s0) * 2 * SKETCH:(s - s0 + 1) * 2 * SKETCH, :]
            for half, value in enumerate((
                prod[:SKETCH, :LINES] + prod[SKETCH:, LINES:],
                prod[SKETCH:, :LINES] - prod[:SKETCH, LINES:],
            )):
                row = s * 2 * SKETCH + half * SKETCH
                put(0, row, value)

    def landed(ref, sem):
        pltpu.make_async_copy(ref, ref, sem).wait()

    def pair(half, q, count):
        span = pl.ds(q, count)
        return remote(part.at[half, span], crecv.at[span], c_send, c_recv, mate)

    for t0 in range(SEGMENTS - 4, -1, -4):
        n = 8 * (t0 // 8 + 1)
        zero = jnp.zeros((n, LINES), jnp.float32)
        accs = [zero] * 8
        for c in range(channels):
            vre = sre[pl.ds(c, n, stride=channels), :]
            vim = sim[pl.ds(c, n, stride=channels), :]
            for a in range(4):
                bre = sre[(t0 + a) * channels + c:(t0 + a) * channels + c + 1, :]
                bim = sim[(t0 + a) * channels + c:(t0 + a) * channels + c + 1, :]
                accs[2 * a] += vre * bre + vim * bim
                accs[2 * a + 1] += vre * bim - vim * bre
        for a in range(4):
            for half in range(2):
                for tile in range(n // 8):
                    row = gram_row(t0 + a, 8 * tile, half)
                    put(1, row, accs[2 * a + half][8 * tile:8 * tile + 8, :])
    pl.semaphore_wait(barrier, units + nz // 2 - 1)
    pair(1 - core, 0, units).start()

    landed(crecv, c_recv)
    for d in far_first:
        u = unit_at(d, 1)
        crecv[u] = crecv[u] + part[core, u]
        remote(crecv.at[u], xrecv.at[d], x_send, x_recv, unit_device(u)).start()
    total = crecv[here] + part[core, here]
    landed(xrecv.at[pl.ds(1, units - 1)], x_recv)
    for d in range(1, units):
        total = total + xrecv[d]
    zall[level] = total
    for e in range(1, nz // 2):
        remote(zall.at[level], zall.at[level], z_send, z_recv, level_device(e)).start()
    landed(zall.at[pl.ds(1, nz // 2 - 1)], z_recv)
    total = zall[0]
    for e in range(1, nz // 2):
        total = total + zall[e]
    full[core, here] = total
    for d in far_first:
        remote(full.at[core, here], full.at[core, here], a_send, a_recv.at[d], unit_device(unit_at(d, 1))).start()
    for d in [0] + far_first:
        u = unit_at(d, -1)
        if d:
            remote(full.at[core, u], full.at[core, u], a_send, a_recv.at[d], unit_device(u)).wait_recv()
        remote(full.at[core, u], full.at[core, u], f_send, f_recv, mate).start()
    landed(full.at[1 - core], f_recv)
    landed(full.at[core], f_send)
    landed(crecv, c_send)
    landed(zall.at[pl.ds(1, nz // 2 - 1)], z_send)
    landed(xrecv.at[pl.ds(1, units - 1)], x_send)
    landed(xrecv.at[pl.ds(1, units - 1)], a_send)
    full_out[...] = full[...]


def all_sums(dims, strain, table, seed):
    nx, ny, nz = dims
    units = nx * ny * 2
    rows = HALF_ROWS // units
    channels = strain.shape[0]
    vmem = pl.BlockSpec(memory_space=pltpu.VMEM)
    dma = pltpu.SemaphoreType.DMA
    spectrum = jax.ShapeDtypeStruct((SEGMENTS * channels, LINES), jnp.float32)
    return pl.pallas_call(
        functools.partial(sum_kernel, dims),
        out_shape=[jax.ShapeDtypeStruct((2, units, rows, LINES), jnp.float32), spectrum, spectrum],
        in_specs=[vmem, vmem, pl.BlockSpec(memory_space=pltpu.SMEM)],
        out_specs=[vmem, vmem, vmem],
        scratch_shapes=[
            pltpu.VMEM((2, units, rows, LINES), jnp.float32),
            pltpu.VMEM((units, rows, LINES), jnp.float32),
            pltpu.VMEM((units, rows, LINES), jnp.float32),
            pltpu.VMEM((nz // 2, rows, LINES), jnp.float32),
            pltpu.VMEM((2, units, rows, LINES), jnp.float32),
        ] + [dma(())] * 7 + [dma((units,)), dma(()), dma(())],
        compiler_params=pltpu.CompilerParams(
            collective_id=0, has_side_effects=True, vmem_limit_bytes=48 * 1024 * 1024
        ),
        name="sums",
    )(strain, table, seed)


def mode_kernel(scaling, root, full, sre, sim, modes, factor, gsum, sksum, px, psum, pdiff, hx, hsum, ssum, gram, rows_x, basis):
    channels = sre.shape[0] // SEGMENTS

    def turned(value):
        return jnp.stack([-value[1], value[0]])

    for t in range(SEGMENTS):
        n = 8 * (t // 8 + 1)
        re = full[1, gram_row(t, 0, 0):gram_row(t, 0, 0) + n, :]
        im = full[1, gram_row(t, 0, 1):gram_row(t, 0, 1) + n, :]
        gsum[0, t, :n, :] = re + im
        gsum[1, t, :n, :] = re - im
    for t in range(SEGMENTS):
        row = t * 2 * SKETCH
        sksum[t] = full[0, row:row + SKETCH, :] + full[0, row + SKETCH:row + 2 * SKETCH, :]

    def sketch_of(t):
        row = t * 2 * SKETCH
        return full[0, row:row + SKETCH, :], full[0, row + SKETCH:row + 2 * SKETCH, :], sksum[t]

    def gram_of(s, t):
        sign = s // 8 <= t // 8
        first, second = (t, s) if sign else (s, t)
        row = gram_row(first, second, 0)
        row_im = gram_row(first, second, 1)
        third = gsum[0 if sign else 1, first, second:second + 1, :]
        return full[1, row:row + 1, :], full[1, row_im:row_im + 1, :], third, sign

    def sums(count, shape, left, right):
        accs = [[jnp.zeros(shape, jnp.float32) for _ in range(4)] for _ in range(count)]
        kinds = [set() for _ in range(count)]
        for s in range(SEGMENTS):
            vre, vim, vsum = right(s)
            for a in range(count):
                lre, lim, third, straight = left(s, a)
                kinds[a].add(straight)
                accs[a][0] = accs[a][0] + lre * vre
                if straight:
                    accs[a][1] = accs[a][1] + lim * vim
                else:
                    accs[a][2] = accs[a][2] + lim * vim
                accs[a][3] = accs[a][3] + third * vsum
        out = []
        for a in range(count):
            prod_re, straight, conjugate, both = accs[a]
            im = both - prod_re
            re = prod_re
            if True in kinds[a]:
                im, re = im - straight, re - straight
            if False in kinds[a]:
                im, re = im + conjugate, re + conjugate
            out.append((re, im))
        return out

    def times_gram(right, scale, store):
        for s0 in range(0, SEGMENTS, 4):
            for a, (re, im) in enumerate(sums(4, (SKETCH, LINES), lambda t, a: gram_of(s0 + a, t), right)):
                store(s0 + a, re if scale is None else re * scale * scale, im if scale is None else im * scale * scale)

    def store_p(s, re, im):
        px[s, 0] = re
        px[s, 1] = im
        psum[s] = re + im
        pdiff[s] = re - im

    def store_h(s, re, im):
        hx[s, 0] = re
        hx[s, 1] = im
        hsum[s] = re + im

    times_gram(sketch_of, scaling, store_p)
    times_gram(lambda t: (px[t, 0], px[t, 1], psum[t]), None, store_h)

    for j0 in range(0, SKETCH, 4):
        k0 = 8 * (j0 // 8)

        def left(s, a):
            j = j0 + a
            return px[s, 0, j:j + 1, :], px[s, 1, j:j + 1, :], pdiff[s, j:j + 1, :], False

        right = lambda s: (hx[s, 0, k0:, :], hx[s, 1, k0:, :], hsum[s, k0:, :])
        for a, (re, im) in enumerate(sums(4, (SKETCH - k0, LINES), left, right)):
            gram[j0 + a, 0, k0:, :] = re
            gram[j0 + a, 1, k0:, :] = im

    ssum[...] = sre[...] + sim[...]
    for j0 in range(0, SKETCH, 4):

        def left(s, a):
            j = j0 + a
            return px[s, 0, j:j + 1, :], px[s, 1, j:j + 1, :], psum[s, j:j + 1, :], True

        def right(s):
            span = slice(s * channels, (s + 1) * channels)
            return sre[span, :], sim[span, :], ssum[span, :]

        for a, (re, im) in enumerate(sums(4, (channels, LINES), left, right)):
            basis[j0 + a, 0] = re
            basis[j0 + a, 1] = im

    for i in range(SKETCH):
        k0 = 8 * (i // 8)
        columns = k0 + lax.broadcasted_iota(jnp.int32, (SKETCH - k0, LINES), 0)
        row = gram[i, :, k0:, :]
        diagonal = jnp.sqrt(gram[i, 0, i:i + 1, :])
        inverse = 1.0 / diagonal
        scaled = row * inverse
        re = jnp.where(columns > i, scaled[0], 0.0)
        re = jnp.where(columns == i, diagonal, re)
        im = jnp.where(columns > i, scaled[1], 0.0)
        value = jnp.stack([re, im])
        if k0:
            factor[0, i, :k0, :] = jnp.zeros((k0, LINES), jnp.float32)
            factor[1, i, :k0, :] = jnp.zeros((k0, LINES), jnp.float32)
        factor[0, i, k0:, :] = re
        factor[1, i, k0:, :] = im
        rows_x[i, :, k0:, :] = value
        mode = basis[i] * inverse
        modes[pl.ds(i, channels, stride=2 * SKETCH), :] = mode[0] * root
        modes[pl.ds(i + SKETCH, channels, stride=2 * SKETCH), :] = mode[1] * root
        other = turned(mode)
        for r in range(i + 1, SKETCH):
            r0 = 8 * (r // 8)
            top_re = rows_x[i, 0, r:r + 1, :]
            top_im = rows_x[i, 1, r:r + 1, :]
            late = value[:, r0 - k0:, :]
            gram[r, :, r0:, :] = gram[r, :, r0:, :] - (top_re * late - top_im * turned(late))
            basis[r] = basis[r] - (top_re * mode + top_im * other)


def finish(full, sre, sim, channels_all):
    channels = sre.shape[0] // SEGMENTS
    vmem = pl.BlockSpec(memory_space=pltpu.VMEM)
    kernel = functools.partial(mode_kernel, 1.0 / (SEGMENTS * channels_all), math.sqrt(channels_all))
    tall = pltpu.VMEM((SEGMENTS, 2, SKETCH, LINES), jnp.float32)
    short = pltpu.VMEM((SEGMENTS, SKETCH, LINES), jnp.float32)
    wide = pltpu.VMEM((SKETCH, 2, SKETCH, LINES), jnp.float32)
    return pl.pallas_call(
        kernel,
        out_shape=[
            jax.ShapeDtypeStruct((channels * 2 * SKETCH, LINES), jnp.float32),
            jax.ShapeDtypeStruct((2, SKETCH, SKETCH, LINES), jnp.float32),
        ],
        in_specs=[vmem] * 3,
        out_specs=[vmem] * 2,
        scratch_shapes=[
            pltpu.VMEM((2, SEGMENTS, SEGMENTS, LINES), jnp.float32), short, tall, short, short, tall, short,
            pltpu.VMEM((SEGMENTS * channels, LINES), jnp.float32),
            wide, wide, pltpu.VMEM((SKETCH, 2, channels, LINES), jnp.float32),
        ],
        compiler_params=pltpu.CompilerParams(vmem_limit_bytes=48 * 1024 * 1024),
        name="modes",
    )(full, sre, sim)


def shards(dims, strain, band_start, sketch_seed):
    channels, samples = strain.shape
    channels_all = channels * lax.axis_size("ch")
    table = dft_table(band_start, samples // SEGMENTS, LINES)
    full, sre, sim = all_sums(dims, strain, table, sketch_seed)
    modes, factor = finish(full.reshape(2, HALF_ROWS, LINES), sre, sim, channels_all)
    return modes.reshape(channels, 2, SKETCH, LINES), factor


def solution(mesh, dims=(4, 4, 16)):
    in_specs = (P("ch", None), P(), P())
    out_specs = (P("ch", None, None, None), P())
    return jax.shard_map(
        functools.partial(shards, dims), mesh=mesh, in_specs=in_specs, out_specs=out_specs, check_vma=False
    )
```

```python
import functools
import math

import jax
import jax.numpy as jnp
from jax import lax
from jax.experimental import pallas as pl
from jax.experimental.pallas import tpu as pltpu
from jax.sharding import PartitionSpec as P

SEGMENTS = 24
LINES = 128
SKETCH = 16
HALF_ROWS = SEGMENTS * 2 * SKETCH
MESH = pl.DeviceIdType.MESH
GROUP = 4


def dft_table(band_start, segment_length, line_count):
    times_idx = jnp.arange(segment_length, dtype=jnp.int32)[:, None]
    line_ids = band_start[0] + jnp.arange(line_count, dtype=jnp.int32)[None, :]
    residues = times_idx * line_ids % segment_length
    phases = 2.0 * math.pi / segment_length * residues.astype(jnp.float32)
    window = 0.5 - 0.5 * jnp.cos(2.0 * math.pi / segment_length * times_idx.astype(jnp.float32))
    weighting = window / math.sqrt(3.0 * segment_length / 8.0)
    return jnp.concatenate(
        [weighting * jnp.cos(phases), -weighting * jnp.sin(phases)], axis=1
    ).astype(jnp.bfloat16)


def sign_block(first_channel, seed, channels, copies, group):
    shape = (group * 2 * SKETCH, group * copies * channels)
    row = lax.broadcasted_iota(jnp.int32, shape, 0)
    col = lax.broadcasted_iota(jnp.int32, shape, 1)
    inside = jnp.zeros(shape, jnp.bool_)
    for g in range(group):
        inside = inside | (
            (row >= g * 2 * SKETCH) & (row < (g + 1) * 2 * SKETCH)
            & (col >= g * copies * channels) & (col < (g + 1) * copies * channels)
        )
    channel = first_channel + jnp.bitwise_and(col, channels - 1)
    half = jnp.bitwise_and(lax.shift_right_logical(row, jnp.full_like(row, 4)), 1)
    column = jnp.bitwise_and(row, SKETCH - 1)
    hashed = (channel * SKETCH + column) * 2 + half + seed * 1000003
    hashed = hashed * -1640531535
    hashed = jnp.bitwise_xor(hashed, lax.shift_right_logical(hashed, jnp.full_like(hashed, 15)))
    hashed = hashed * 2146121005
    hashed = jnp.bitwise_xor(hashed, lax.shift_right_logical(hashed, jnp.full_like(hashed, 13)))
    bits = jnp.bitwise_and(lax.shift_right_logical(hashed, jnp.full_like(hashed, 7)), 1)
    return jnp.where(inside, (1 - 2 * bits).astype(jnp.float32), 0.0)


def gram_row(t, s, part):
    block = t // 8
    return 8 * (0, 16, 48)[block] + (t % 8) * 16 * (block + 1) + part * 8 * (block + 1) + s


def sum_kernel(dims, strain, table, seed, full_out, sre, sim,
               part, crecv, xrecv, zall, full,
               c_send, c_recv, x_send, x_recv, z_send, z_recv, a_send, a_recv, f_send, f_recv):
    nx, ny, nz = dims
    units = nx * ny * 2
    rows = HALF_ROWS // units
    channels = strain.shape[0]
    length = table.shape[0]

    me = lax.axis_index("ch")
    core = lax.rem(me, 2)
    z = lax.rem(lax.div(me, 2), nz)
    p = lax.div(me, 2 * nz)
    x, y = lax.div(p, ny), lax.rem(p, ny)
    odd, level = lax.rem(z, 2), lax.div(z, 2)
    mate = me + 1 - 2 * core
    here = p * 2 + odd

    def unit_at(d, sign):
        dx, dy, flip = d // 2 // ny, d // 2 % ny, d % 2
        qx = lax.rem(x + (dx if sign > 0 else nx - dx), nx)
        qy = lax.rem(y + (dy if sign > 0 else ny - dy), ny)
        return (qx * ny + qy) * 2 + (1 - odd if flip else odd)

    def hops(d):
        dx, dy = d // 2 // ny, d // 2 % ny
        return min(dx, nx - dx) + min(dy, ny - dy) + d % 2

    level_order = sorted(range(1, nz // 2), key=lambda e: (-min(e, nz // 2 - e), e))
    far_first = sorted(range(1, units), key=lambda d: (-hops(d), d))

    def unit_device(u):
        return lax.div(u, 2) * (2 * nz) + (level * 2 + lax.rem(u, 2)) * 2 + core

    def level_device(e):
        return p * (2 * nz) + (lax.rem(level + e, nz // 2) * 2 + odd) * 2 + core

    barrier = pltpu.get_barrier_semaphore()
    for e in level_order:
        pl.semaphore_signal(barrier, inc=1, device_id=(level_device(e),), device_id_type=MESH)
    for d in far_first:
        pl.semaphore_signal(barrier, inc=1, device_id=(unit_device(unit_at(d, 1)),), device_id_type=MESH)
    pl.semaphore_signal(barrier, inc=1, device_id=(mate,), device_id_type=MESH)

    def put(half, row, value):
        for r in range(row, row + value.shape[0], 8):
            part[half, r // rows, r % rows:r % rows + 8, :] = value[r - row:r - row + 8, :]

    def remote(src, dst, send, recv, device):
        return pltpu.make_async_remote_copy(
            src_ref=src, dst_ref=dst, send_sem=send, recv_sem=recv, device_id=(device,), device_id_type=MESH
        )

    flat = jnp.concatenate([strain[:, s * length:(s + 1) * length] for s in range(SEGMENTS)], axis=0)
    both = jnp.dot(flat, table[...], preferred_element_type=jnp.float32)
    sre[...] = both[:, :LINES]
    sim[...] = both[:, LINES:]

    signs = sign_block(me * channels, seed[0], channels, 3, GROUP).astype(jnp.bfloat16)
    for s0 in range(0, SEGMENTS, GROUP):
        terms = []
        for s in range(s0, s0 + GROUP):
            both = jnp.concatenate(
                [sre[s * channels:(s + 1) * channels, :], sim[s * channels:(s + 1) * channels, :]], axis=1
            )
            high = both.astype(jnp.bfloat16)
            rest = both - high.astype(jnp.float32)
            middle = rest.astype(jnp.bfloat16)
            low = (rest - middle.astype(jnp.float32)).astype(jnp.bfloat16)
            terms += [high, middle, low]
        prods = jnp.dot(signs, jnp.concatenate(terms, axis=0), preferred_element_type=jnp.float32)
        for s in range(s0, s0 + GROUP):
            prod = prods[(s - s0) * 2 * SKETCH:(s - s0 + 1) * 2 * SKETCH, :]
            for half, value in enumerate((
                prod[:SKETCH, :LINES] + prod[SKETCH:, LINES:],
                prod[SKETCH:, :LINES] - prod[:SKETCH, LINES:],
            )):
                row = s * 2 * SKETCH + half * SKETCH
                put(0, row, value)

    def landed(ref, sem):
        pltpu.make_async_copy(ref, ref, sem).wait()

    def pair(half, q, count):
        span = pl.ds(q, count)
        return remote(part.at[half, span], crecv.at[span], c_send, c_recv, mate)

    for t0 in range(SEGMENTS - 4, -1, -4):
        n = 8 * (t0 // 8 + 1)
        zero = jnp.zeros((n, LINES), jnp.float32)
        accs = [zero] * 8
        for c in range(channels):
            vre = sre[pl.ds(c, n, stride=channels), :]
            vim = sim[pl.ds(c, n, stride=channels), :]
            for a in range(4):
                bre = sre[(t0 + a) * channels + c:(t0 + a) * channels + c + 1, :]
                bim = sim[(t0 + a) * channels + c:(t0 + a) * channels + c + 1, :]
                accs[2 * a] += vre * bre + vim * bim
                accs[2 * a + 1] += vre * bim - vim * bre
        for a in range(4):
            for half in range(2):
                for tile in range(n // 8):
                    row = gram_row(t0 + a, 8 * tile, half)
                    put(1, row, accs[2 * a + half][8 * tile:8 * tile + 8, :])
    pl.semaphore_wait(barrier, units + nz // 2 - 1)
    pair(1 - core, 0, units).start()

    landed(crecv, c_recv)
    for d in far_first:
        u = unit_at(d, 1)
        crecv[u] = crecv[u] + part[core, u]
        remote(crecv.at[u], xrecv.at[d], x_send, x_recv, unit_device(u)).start()
    total = crecv[here] + part[core, here]
    landed(xrecv.at[pl.ds(1, units - 1)], x_recv)
    for d in range(1, units):
        total = total + xrecv[d]
    zall[level] = total
    for e in level_order:
        remote(zall.at[level], zall.at[level], z_send, z_recv, level_device(e)).start()
    landed(zall.at[pl.ds(1, nz // 2 - 1)], z_recv)
    total = zall[0]
    for e in range(1, nz // 2):
        total = total + zall[e]
    full[core, here] = total
    for d in far_first:
        remote(full.at[core, here], full.at[core, here], a_send, a_recv.at[d], unit_device(unit_at(d, 1))).start()
    for d in [0] + far_first:
        u = unit_at(d, -1)
        if d:
            remote(full.at[core, u], full.at[core, u], a_send, a_recv.at[d], unit_device(u)).wait_recv()
        remote(full.at[core, u], full.at[core, u], f_send, f_recv, mate).start()
    landed(full.at[1 - core], f_recv)
    landed(full.at[core], f_send)
    landed(crecv, c_send)
    landed(zall.at[pl.ds(1, nz // 2 - 1)], z_send)
    landed(xrecv.at[pl.ds(1, units - 1)], x_send)
    landed(xrecv.at[pl.ds(1, units - 1)], a_send)
    full_out[...] = full[...]


def all_sums(dims, strain, table, seed):
    nx, ny, nz = dims
    units = nx * ny * 2
    rows = HALF_ROWS // units
    channels = strain.shape[0]
    vmem = pl.BlockSpec(memory_space=pltpu.VMEM)
    dma = pltpu.SemaphoreType.DMA
    spectrum = jax.ShapeDtypeStruct((SEGMENTS * channels, LINES), jnp.float32)
    return pl.pallas_call(
        functools.partial(sum_kernel, dims),
        out_shape=[jax.ShapeDtypeStruct((2, units, rows, LINES), jnp.float32), spectrum, spectrum],
        in_specs=[vmem, vmem, pl.BlockSpec(memory_space=pltpu.SMEM)],
        out_specs=[vmem, vmem, vmem],
        scratch_shapes=[
            pltpu.VMEM((2, units, rows, LINES), jnp.float32),
            pltpu.VMEM((units, rows, LINES), jnp.float32),
            pltpu.VMEM((units, rows, LINES), jnp.float32),
            pltpu.VMEM((nz // 2, rows, LINES), jnp.float32),
            pltpu.VMEM((2, units, rows, LINES), jnp.float32),
        ] + [dma(())] * 7 + [dma((units,)), dma(()), dma(())],
        compiler_params=pltpu.CompilerParams(
            collective_id=0, has_side_effects=True, vmem_limit_bytes=48 * 1024 * 1024
        ),
        name="sums",
    )(strain, table, seed)


def mode_kernel(scaling, root, full, sre, sim, modes, factor, gsum, sksum, px, psum, pdiff, hx, hsum, ssum, gram, rows_x, basis):
    channels = sre.shape[0] // SEGMENTS

    def turned(value):
        return jnp.stack([-value[1], value[0]])

    for t in range(SEGMENTS):
        n = 8 * (t // 8 + 1)
        re = full[1, gram_row(t, 0, 0):gram_row(t, 0, 0) + n, :]
        im = full[1, gram_row(t, 0, 1):gram_row(t, 0, 1) + n, :]
        gsum[0, t, :n, :] = re + im
        gsum[1, t, :n, :] = re - im
    for t in range(SEGMENTS):
        row = t * 2 * SKETCH
        sksum[t] = full[0, row:row + SKETCH, :] + full[0, row + SKETCH:row + 2 * SKETCH, :]

    def sketch_of(t):
        row = t * 2 * SKETCH
        return full[0, row:row + SKETCH, :], full[0, row + SKETCH:row + 2 * SKETCH, :], sksum[t]

    def gram_of(s, t):
        sign = s // 8 <= t // 8
        first, second = (t, s) if sign else (s, t)
        row = gram_row(first, second, 0)
        row_im = gram_row(first, second, 1)
        third = gsum[0 if sign else 1, first, second:second + 1, :]
        return full[1, row:row + 1, :], full[1, row_im:row_im + 1, :], third, sign

    def sums(count, shape, left, right):
        accs = [[jnp.zeros(shape, jnp.float32) for _ in range(4)] for _ in range(count)]
        kinds = [set() for _ in range(count)]
        for s in range(SEGMENTS):
            vre, vim, vsum = right(s)
            for a in range(count):
                lre, lim, third, straight = left(s, a)
                kinds[a].add(straight)
                accs[a][0] = accs[a][0] + lre * vre
                if straight:
                    accs[a][1] = accs[a][1] + lim * vim
                else:
                    accs[a][2] = accs[a][2] + lim * vim
                accs[a][3] = accs[a][3] + third * vsum
        out = []
        for a in range(count):
            prod_re, straight, conjugate, both = accs[a]
            im = both - prod_re
            re = prod_re
            if True in kinds[a]:
                im, re = im - straight, re - straight
            if False in kinds[a]:
                im, re = im + conjugate, re + conjugate
            out.append((re, im))
        return out

    def times_gram(right, scale, store):
        for s0 in range(0, SEGMENTS, 4):
            for a, (re, im) in enumerate(sums(4, (SKETCH, LINES), lambda t, a: gram_of(s0 + a, t), right)):
                store(s0 + a, re if scale is None else re * scale * scale, im if scale is None else im * scale * scale)

    def store_p(s, re, im):
        px[s, 0] = re
        px[s, 1] = im
        psum[s] = re + im
        pdiff[s] = re - im

    def store_h(s, re, im):
        hx[s, 0] = re
        hx[s, 1] = im
        hsum[s] = re + im

    times_gram(sketch_of, scaling, store_p)
    times_gram(lambda t: (px[t, 0], px[t, 1], psum[t]), None, store_h)

    for j0 in range(0, SKETCH, 4):
        k0 = 8 * (j0 // 8)

        def left(s, a):
            j = j0 + a
            return px[s, 0, j:j + 1, :], px[s, 1, j:j + 1, :], pdiff[s, j:j + 1, :], False

        right = lambda s: (hx[s, 0, k0:, :], hx[s, 1, k0:, :], hsum[s, k0:, :])
        for a, (re, im) in enumerate(sums(4, (SKETCH - k0, LINES), left, right)):
            gram[j0 + a, 0, k0:, :] = re
            gram[j0 + a, 1, k0:, :] = im

    ssum[...] = sre[...] + sim[...]
    for j0 in range(0, SKETCH, 4):

        def left(s, a):
            j = j0 + a
            return px[s, 0, j:j + 1, :], px[s, 1, j:j + 1, :], psum[s, j:j + 1, :], True

        def right(s):
            span = slice(s * channels, (s + 1) * channels)
            return sre[span, :], sim[span, :], ssum[span, :]

        for a, (re, im) in enumerate(sums(4, (channels, LINES), left, right)):
            basis[j0 + a, 0] = re
            basis[j0 + a, 1] = im

    for i in range(SKETCH):
        k0 = 8 * (i // 8)
        columns = k0 + lax.broadcasted_iota(jnp.int32, (SKETCH - k0, LINES), 0)
        row = gram[i, :, k0:, :]
        diagonal = jnp.sqrt(gram[i, 0, i:i + 1, :])
        inverse = 1.0 / diagonal
        scaled = row * inverse
        re = jnp.where(columns > i, scaled[0], 0.0)
        re = jnp.where(columns == i, diagonal, re)
        im = jnp.where(columns > i, scaled[1], 0.0)
        value = jnp.stack([re, im])
        if k0:
            factor[0, i, :k0, :] = jnp.zeros((k0, LINES), jnp.float32)
            factor[1, i, :k0, :] = jnp.zeros((k0, LINES), jnp.float32)
        factor[0, i, k0:, :] = re
        factor[1, i, k0:, :] = im
        rows_x[i, :, k0:, :] = value
        mode = basis[i] * inverse
        modes[pl.ds(i, channels, stride=2 * SKETCH), :] = mode[0] * root
        modes[pl.ds(i + SKETCH, channels, stride=2 * SKETCH), :] = mode[1] * root
        other = turned(mode)
        for r in range(i + 1, SKETCH):
            r0 = 8 * (r // 8)
            top_re = rows_x[i, 0, r:r + 1, :]
            top_im = rows_x[i, 1, r:r + 1, :]
            late = value[:, r0 - k0:, :]
            gram[r, :, r0:, :] = gram[r, :, r0:, :] - (top_re * late - top_im * turned(late))
            basis[r] = basis[r] - (top_re * mode + top_im * other)


def finish(full, sre, sim, channels_all):
    channels = sre.shape[0] // SEGMENTS
    vmem = pl.BlockSpec(memory_space=pltpu.VMEM)
    kernel = functools.partial(mode_kernel, 1.0 / (SEGMENTS * channels_all), math.sqrt(channels_all))
    tall = pltpu.VMEM((SEGMENTS, 2, SKETCH, LINES), jnp.float32)
    short = pltpu.VMEM((SEGMENTS, SKETCH, LINES), jnp.float32)
    wide = pltpu.VMEM((SKETCH, 2, SKETCH, LINES), jnp.float32)
    return pl.pallas_call(
        kernel,
        out_shape=[
            jax.ShapeDtypeStruct((channels * 2 * SKETCH, LINES), jnp.float32),
            jax.ShapeDtypeStruct((2, SKETCH, SKETCH, LINES), jnp.float32),
        ],
        in_specs=[vmem] * 3,
        out_specs=[vmem] * 2,
        scratch_shapes=[
            pltpu.VMEM((2, SEGMENTS, SEGMENTS, LINES), jnp.float32), short, tall, short, short, tall, short,
            pltpu.VMEM((SEGMENTS * channels, LINES), jnp.float32),
            wide, wide, pltpu.VMEM((SKETCH, 2, channels, LINES), jnp.float32),
        ],
        compiler_params=pltpu.CompilerParams(vmem_limit_bytes=48 * 1024 * 1024),
        name="modes",
    )(full, sre, sim)


def shards(dims, strain, band_start, sketch_seed):
    channels, samples = strain.shape
    channels_all = channels * lax.axis_size("ch")
    table = dft_table(band_start, samples // SEGMENTS, LINES)
    full, sre, sim = all_sums(dims, strain, table, sketch_seed)
    modes, factor = finish(full.reshape(2, HALF_ROWS, LINES), sre, sim, channels_all)
    return modes.reshape(channels, 2, SKETCH, LINES), factor


def solution(mesh, dims=(4, 4, 16)):
    in_specs = (P("ch", None), P(), P())
    out_specs = (P("ch", None, None, None), P())
    return jax.shard_map(
        functools.partial(shards, dims), mesh=mesh, in_specs=in_specs, out_specs=out_specs, check_vma=False
    )
```

```python
import functools
import math

import jax
import jax.numpy as jnp
from jax import lax
from jax.experimental import pallas as pl
from jax.experimental.pallas import tpu as pltpu
from jax.sharding import PartitionSpec as P

SEGMENTS = 24
LINES = 128
SKETCH = 16
HALF_ROWS = SEGMENTS * 2 * SKETCH
MESH = pl.DeviceIdType.MESH
GROUP = 4


def dft_table(band_start, segment_length, line_count):
    times_idx = jnp.arange(segment_length, dtype=jnp.int32)[:, None]
    line_ids = band_start[0] + jnp.arange(line_count, dtype=jnp.int32)[None, :]
    residues = times_idx * line_ids % segment_length
    phases = 2.0 * math.pi / segment_length * residues.astype(jnp.float32)
    window = 0.5 - 0.5 * jnp.cos(2.0 * math.pi / segment_length * times_idx.astype(jnp.float32))
    weighting = window / math.sqrt(3.0 * segment_length / 8.0)
    return jnp.concatenate(
        [weighting * jnp.cos(phases), -weighting * jnp.sin(phases)], axis=1
    ).astype(jnp.bfloat16)


def sign_block(first_channel, seed, channels, copies, group):
    shape = (group * 2 * SKETCH, group * copies * channels)
    row = lax.broadcasted_iota(jnp.int32, shape, 0)
    col = lax.broadcasted_iota(jnp.int32, shape, 1)
    inside = jnp.zeros(shape, jnp.bool_)
    for g in range(group):
        inside = inside | (
            (row >= g * 2 * SKETCH) & (row < (g + 1) * 2 * SKETCH)
            & (col >= g * copies * channels) & (col < (g + 1) * copies * channels)
        )
    channel = first_channel + jnp.bitwise_and(col, channels - 1)
    half = jnp.bitwise_and(lax.shift_right_logical(row, jnp.full_like(row, 4)), 1)
    column = jnp.bitwise_and(row, SKETCH - 1)
    hashed = (channel * SKETCH + column) * 2 + half + seed * 1000003
    hashed = hashed * -1640531535
    hashed = jnp.bitwise_xor(hashed, lax.shift_right_logical(hashed, jnp.full_like(hashed, 15)))
    hashed = hashed * 2146121005
    hashed = jnp.bitwise_xor(hashed, lax.shift_right_logical(hashed, jnp.full_like(hashed, 13)))
    bits = jnp.bitwise_and(lax.shift_right_logical(hashed, jnp.full_like(hashed, 7)), 1)
    return jnp.where(inside, (1 - 2 * bits).astype(jnp.float32), 0.0)


def gram_row(t, s, part):
    block = t // 8
    return 8 * (0, 16, 48)[block] + (t % 8) * 16 * (block + 1) + part * 8 * (block + 1) + s


def sum_kernel(dims, strain, table, seed, full_out, sre, sim,
               part, crecv, xrecv, zall, full,
               c_send, c_recv, x_send, x_recv, z_send, z_recv, a_send, a_recv, f_send, f_recv):
    nx, ny, nz = dims
    units = nx * ny * 2
    rows = HALF_ROWS // units
    channels = strain.shape[0]
    length = table.shape[0]

    me = lax.axis_index("ch")
    core = lax.rem(me, 2)
    z = lax.rem(lax.div(me, 2), nz)
    p = lax.div(me, 2 * nz)
    x, y = lax.div(p, ny), lax.rem(p, ny)
    odd, level = lax.rem(z, 2), lax.div(z, 2)
    mate = me + 1 - 2 * core
    here = p * 2 + odd

    def unit_at(d, sign):
        dx, dy, flip = d // 2 // ny, d // 2 % ny, d % 2
        qx = lax.rem(x + (dx if sign > 0 else nx - dx), nx)
        qy = lax.rem(y + (dy if sign > 0 else ny - dy), ny)
        return (qx * ny + qy) * 2 + (1 - odd if flip else odd)

    def hops(d):
        dx, dy = d // 2 // ny, d // 2 % ny
        return min(dx, nx - dx) + min(dy, ny - dy) + d % 2

    level_order = sorted(range(1, nz // 2), key=lambda e: (-min(e, nz // 2 - e), e))
    far_first = sorted(range(1, units), key=lambda d: (-hops(d), d))

    def unit_device(u):
        return lax.div(u, 2) * (2 * nz) + (level * 2 + lax.rem(u, 2)) * 2 + core

    def level_device(e):
        return p * (2 * nz) + (lax.rem(level + e, nz // 2) * 2 + odd) * 2 + core

    barrier = pltpu.get_barrier_semaphore()
    for e in level_order:
        pl.semaphore_signal(barrier, inc=1, device_id=(level_device(e),), device_id_type=MESH)
    for d in far_first:
        pl.semaphore_signal(barrier, inc=1, device_id=(unit_device(unit_at(d, 1)),), device_id_type=MESH)
    pl.semaphore_signal(barrier, inc=1, device_id=(mate,), device_id_type=MESH)

    def put(half, row, value):
        for r in range(row, row + value.shape[0], 8):
            part[half, r // rows, r % rows:r % rows + 8, :] = value[r - row:r - row + 8, :]

    def remote(src, dst, send, recv, device):
        return pltpu.make_async_remote_copy(
            src_ref=src, dst_ref=dst, send_sem=send, recv_sem=recv, device_id=(device,), device_id_type=MESH
        )

    flat = jnp.concatenate([strain[:, s * length:(s + 1) * length] for s in range(SEGMENTS)], axis=0)
    both = jnp.dot(flat, table[...], preferred_element_type=jnp.float32)
    sre[...] = both[:, :LINES]
    sim[...] = both[:, LINES:]

    signs = sign_block(me * channels, seed[0], channels, 3, GROUP).astype(jnp.bfloat16)
    for s0 in range(0, SEGMENTS, GROUP):
        terms = []
        for s in range(s0, s0 + GROUP):
            both = jnp.concatenate(
                [sre[s * channels:(s + 1) * channels, :], sim[s * channels:(s + 1) * channels, :]], axis=1
            )
            high = both.astype(jnp.bfloat16)
            rest = both - high.astype(jnp.float32)
            middle = rest.astype(jnp.bfloat16)
            low = (rest - middle.astype(jnp.float32)).astype(jnp.bfloat16)
            terms += [high, middle, low]
        prods = jnp.dot(signs, jnp.concatenate(terms, axis=0), preferred_element_type=jnp.float32)
        for s in range(s0, s0 + GROUP):
            prod = prods[(s - s0) * 2 * SKETCH:(s - s0 + 1) * 2 * SKETCH, :]
            for half, value in enumerate((
                prod[:SKETCH, :LINES] + prod[SKETCH:, LINES:],
                prod[SKETCH:, :LINES] - prod[:SKETCH, LINES:],
            )):
                row = s * 2 * SKETCH + half * SKETCH
                put(0, row, value)

    def landed(ref, sem):
        pltpu.make_async_copy(ref, ref, sem).wait()

    def pair(half, q, count):
        span = pl.ds(q, count)
        return remote(part.at[half, span], crecv.at[span], c_send, c_recv, mate)

    for t0 in range(SEGMENTS - 4, -1, -4):
        n = 8 * (t0 // 8 + 1)
        zero = jnp.zeros((n, LINES), jnp.float32)
        accs = [zero] * 12
        for c in range(channels):
            vre = sre[pl.ds(c, n, stride=channels), :]
            vim = sim[pl.ds(c, n, stride=channels), :]
            vdiff = vre - vim
            for a in range(4):
                bre = sre[(t0 + a) * channels + c:(t0 + a) * channels + c + 1, :]
                bim = sim[(t0 + a) * channels + c:(t0 + a) * channels + c + 1, :]
                accs[3 * a] += vre * bre
                accs[3 * a + 1] += vim * bim
                accs[3 * a + 2] += vdiff * (bre + bim)
        for a in range(4):
            first, second, third = accs[3 * a:3 * a + 3]
            value = (first + second, third - first + second)
            for half in range(2):
                for tile in range(n // 8):
                    row = gram_row(t0 + a, 8 * tile, half)
                    put(1, row, value[half][8 * tile:8 * tile + 8, :])
    pl.semaphore_wait(barrier, units + nz // 2 - 1)
    pair(1 - core, 0, units).start()

    landed(crecv, c_recv)
    for d in far_first:
        u = unit_at(d, 1)
        crecv[u] = crecv[u] + part[core, u]
        remote(crecv.at[u], xrecv.at[d], x_send, x_recv, unit_device(u)).start()
    total = crecv[here] + part[core, here]
    landed(xrecv.at[pl.ds(1, units - 1)], x_recv)
    for d in range(1, units):
        total = total + xrecv[d]
    zall[level] = total
    for e in level_order:
        remote(zall.at[level], zall.at[level], z_send, z_recv, level_device(e)).start()
    landed(zall.at[pl.ds(1, nz // 2 - 1)], z_recv)
    total = zall[0]
    for e in range(1, nz // 2):
        total = total + zall[e]
    full[core, here] = total
    for d in far_first:
        remote(full.at[core, here], full.at[core, here], a_send, a_recv.at[d], unit_device(unit_at(d, 1))).start()
    for d in [0] + far_first:
        u = unit_at(d, -1)
        if d:
            remote(full.at[core, u], full.at[core, u], a_send, a_recv.at[d], unit_device(u)).wait_recv()
        remote(full.at[core, u], full.at[core, u], f_send, f_recv, mate).start()
    full_out[core] = full[core]
    landed(full.at[1 - core], f_recv)
    landed(full.at[core], f_send)
    landed(crecv, c_send)
    landed(zall.at[pl.ds(1, nz // 2 - 1)], z_send)
    landed(xrecv.at[pl.ds(1, units - 1)], x_send)
    landed(xrecv.at[pl.ds(1, units - 1)], a_send)
    full_out[1 - core] = full[1 - core]


def all_sums(dims, strain, table, seed):
    nx, ny, nz = dims
    units = nx * ny * 2
    rows = HALF_ROWS // units
    channels = strain.shape[0]
    vmem = pl.BlockSpec(memory_space=pltpu.VMEM)
    dma = pltpu.SemaphoreType.DMA
    spectrum = jax.ShapeDtypeStruct((SEGMENTS * channels, LINES), jnp.float32)
    return pl.pallas_call(
        functools.partial(sum_kernel, dims),
        out_shape=[jax.ShapeDtypeStruct((2, units, rows, LINES), jnp.float32), spectrum, spectrum],
        in_specs=[vmem, vmem, pl.BlockSpec(memory_space=pltpu.SMEM)],
        out_specs=[vmem, vmem, vmem],
        scratch_shapes=[
            pltpu.VMEM((2, units, rows, LINES), jnp.float32),
            pltpu.VMEM((units, rows, LINES), jnp.float32),
            pltpu.VMEM((units, rows, LINES), jnp.float32),
            pltpu.VMEM((nz // 2, rows, LINES), jnp.float32),
            pltpu.VMEM((2, units, rows, LINES), jnp.float32),
        ] + [dma(())] * 7 + [dma((units,)), dma(()), dma(())],
        compiler_params=pltpu.CompilerParams(
            collective_id=0, has_side_effects=True, vmem_limit_bytes=48 * 1024 * 1024
        ),
        name="sums",
    )(strain, table, seed)


def mode_kernel(scaling, root, full, sre, sim, modes, factor, gsum, sksum, px, psum, pdiff, hx, hsum, ssum, gram, rows_x, basis):
    channels = sre.shape[0] // SEGMENTS

    def turned(value):
        return jnp.stack([-value[1], value[0]])

    for t in range(SEGMENTS):
        n = 8 * (t // 8 + 1)
        re = full[1, gram_row(t, 0, 0):gram_row(t, 0, 0) + n, :]
        im = full[1, gram_row(t, 0, 1):gram_row(t, 0, 1) + n, :]
        gsum[0, t, :n, :] = re + im
        gsum[1, t, :n, :] = re - im
    for t in range(SEGMENTS):
        row = t * 2 * SKETCH
        sksum[t] = full[0, row:row + SKETCH, :] + full[0, row + SKETCH:row + 2 * SKETCH, :]

    def sketch_of(t):
        row = t * 2 * SKETCH
        return full[0, row:row + SKETCH, :], full[0, row + SKETCH:row + 2 * SKETCH, :], sksum[t]

    def gram_of(s, t):
        sign = s // 8 <= t // 8
        first, second = (t, s) if sign else (s, t)
        row = gram_row(first, second, 0)
        row_im = gram_row(first, second, 1)
        third = gsum[0 if sign else 1, first, second:second + 1, :]
        return full[1, row:row + 1, :], full[1, row_im:row_im + 1, :], third, sign

    def sums(count, shape, left, right):
        accs = [[jnp.zeros(shape, jnp.float32) for _ in range(4)] for _ in range(count)]
        kinds = [set() for _ in range(count)]
        for s in range(SEGMENTS):
            vre, vim, vsum = right(s)
            for a in range(count):
                lre, lim, third, straight = left(s, a)
                kinds[a].add(straight)
                accs[a][0] = accs[a][0] + lre * vre
                if straight:
                    accs[a][1] = accs[a][1] + lim * vim
                else:
                    accs[a][2] = accs[a][2] + lim * vim
                accs[a][3] = accs[a][3] + third * vsum
        out = []
        for a in range(count):
            prod_re, straight, conjugate, both = accs[a]
            im = both - prod_re
            re = prod_re
            if True in kinds[a]:
                im, re = im - straight, re - straight
            if False in kinds[a]:
                im, re = im + conjugate, re + conjugate
            out.append((re, im))
        return out

    def times_gram(right, scale, store):
        for s0 in range(0, SEGMENTS, 4):
            for a, (re, im) in enumerate(sums(4, (SKETCH, LINES), lambda t, a: gram_of(s0 + a, t), right)):
                store(s0 + a, re if scale is None else re * scale * scale, im if scale is None else im * scale * scale)

    def store_p(s, re, im):
        px[s, 0] = re
        px[s, 1] = im
        psum[s] = re + im
        pdiff[s] = re - im

    def store_h(s, re, im):
        hx[s, 0] = re
        hx[s, 1] = im
        hsum[s] = re + im

    times_gram(sketch_of, scaling, store_p)
    times_gram(lambda t: (px[t, 0], px[t, 1], psum[t]), None, store_h)

    for j0 in range(0, SKETCH, 4):
        k0 = 8 * (j0 // 8)

        def left(s, a):
            j = j0 + a
            return px[s, 0, j:j + 1, :], px[s, 1, j:j + 1, :], pdiff[s, j:j + 1, :], False

        right = lambda s: (hx[s, 0, k0:, :], hx[s, 1, k0:, :], hsum[s, k0:, :])
        for a, (re, im) in enumerate(sums(4, (SKETCH - k0, LINES), left, right)):
            gram[j0 + a, 0, k0:, :] = re
            gram[j0 + a, 1, k0:, :] = im

    ssum[...] = sre[...] + sim[...]
    for j0 in range(0, SKETCH, 4):

        def left(s, a):
            j = j0 + a
            return px[s, 0, j:j + 1, :], px[s, 1, j:j + 1, :], psum[s, j:j + 1, :], True

        def right(s):
            span = slice(s * channels, (s + 1) * channels)
            return sre[span, :], sim[span, :], ssum[span, :]

        for a, (re, im) in enumerate(sums(4, (channels, LINES), left, right)):
            basis[j0 + a, 0] = re
            basis[j0 + a, 1] = im

    for i in range(SKETCH):
        k0 = 8 * (i // 8)
        columns = k0 + lax.broadcasted_iota(jnp.int32, (SKETCH - k0, LINES), 0)
        row = gram[i, :, k0:, :]
        diagonal = jnp.sqrt(gram[i, 0, i:i + 1, :])
        inverse = 1.0 / diagonal
        scaled = row * inverse
        re = jnp.where(columns > i, scaled[0], 0.0)
        re = jnp.where(columns == i, diagonal, re)
        im = jnp.where(columns > i, scaled[1], 0.0)
        value = jnp.stack([re, im])
        if k0:
            factor[0, i, :k0, :] = jnp.zeros((k0, LINES), jnp.float32)
            factor[1, i, :k0, :] = jnp.zeros((k0, LINES), jnp.float32)
        factor[0, i, k0:, :] = re
        factor[1, i, k0:, :] = im
        rows_x[i, :, k0:, :] = value
        mode = basis[i] * inverse
        modes[pl.ds(i, channels, stride=2 * SKETCH), :] = mode[0] * root
        modes[pl.ds(i + SKETCH, channels, stride=2 * SKETCH), :] = mode[1] * root
        other = turned(mode)
        for r in range(i + 1, SKETCH):
            r0 = 8 * (r // 8)
            top_re = rows_x[i, 0, r:r + 1, :]
            top_im = rows_x[i, 1, r:r + 1, :]
            late = value[:, r0 - k0:, :]
            gram[r, :, r0:, :] = gram[r, :, r0:, :] - (top_re * late - top_im * turned(late))
            basis[r] = basis[r] - (top_re * mode + top_im * other)


def finish(full, sre, sim, channels_all):
    channels = sre.shape[0] // SEGMENTS
    vmem = pl.BlockSpec(memory_space=pltpu.VMEM)
    kernel = functools.partial(mode_kernel, 1.0 / (SEGMENTS * channels_all), math.sqrt(channels_all))
    tall = pltpu.VMEM((SEGMENTS, 2, SKETCH, LINES), jnp.float32)
    short = pltpu.VMEM((SEGMENTS, SKETCH, LINES), jnp.float32)
    wide = pltpu.VMEM((SKETCH, 2, SKETCH, LINES), jnp.float32)
    return pl.pallas_call(
        kernel,
        out_shape=[
            jax.ShapeDtypeStruct((channels * 2 * SKETCH, LINES), jnp.float32),
            jax.ShapeDtypeStruct((2, SKETCH, SKETCH, LINES), jnp.float32),
        ],
        in_specs=[vmem] * 3,
        out_specs=[vmem] * 2,
        scratch_shapes=[
            pltpu.VMEM((2, SEGMENTS, SEGMENTS, LINES), jnp.float32), short, tall, short, short, tall, short,
            pltpu.VMEM((SEGMENTS * channels, LINES), jnp.float32),
            wide, wide, pltpu.VMEM((SKETCH, 2, channels, LINES), jnp.float32),
        ],
        compiler_params=pltpu.CompilerParams(vmem_limit_bytes=48 * 1024 * 1024),
        name="modes",
    )(full, sre, sim)


def shards(dims, strain, band_start, sketch_seed):
    channels, samples = strain.shape
    channels_all = channels * lax.axis_size("ch")
    table = dft_table(band_start, samples // SEGMENTS, LINES)
    full, sre, sim = all_sums(dims, strain, table, sketch_seed)
    modes, factor = finish(full.reshape(2, HALF_ROWS, LINES), sre, sim, channels_all)
    return modes.reshape(channels, 2, SKETCH, LINES), factor


def solution(mesh, dims=(4, 4, 16)):
    in_specs = (P("ch", None), P(), P())
    out_specs = (P("ch", None, None, None), P())
    return jax.shard_map(
        functools.partial(shards, dims), mesh=mesh, in_specs=in_specs, out_specs=out_specs, check_vma=False
    )
```
